32 devices in a mesh: gx: 8 (over y, x, core), gy: 4 (over z).
Axes of the slice: x: 2, y: 2, z: 4, core: 2. Of those that a mesh axis runs over, the one named last changes fastest.
Arguments:
- saved_mid: bfloat16 [384, 128, 256], P('gx', 'gy'), may hold values from -6 to 6
- out_grad: bfloat16 [384, 128, 256], P('gx', 'gy'), may hold values from -6 to 6
- expert_weight: bfloat16 [10, 9, 256, 256], replicated, may hold values from -0.125 to 0.125
- routes: int32 [24, 8, 4], P('gx', 'gy'), may hold values from 0 to 7, all different within a row
- gates: float32 [24, 8, 6], P('gx', 'gy'), may hold values from 0.5 to 1.5
- band_matrix: bfloat16 [16, 256, 256], replicated, may hold values from -0.375 to 0.375
- band_ids: int32 [64, 32], replicated, may hold values from 0 to 15
Outputs:
- field_grad: bfloat16 [384, 128, 256], P('gx', 'gy')
The draws below stay inside these ranges and needn't reach their ends.
Inputs may be any that keep to these rules, and one draw needn't show every extreme that they name: `routes`: each tile names 4 different routed experts.
All inputs are finite; a program needn't handle non-finite values.
Results may differ from the reference program's by a relative error of at most 0.0095.
Values may be sent and summed in bfloat16 or wider, within the bound.
No kernel may reach another device: no remote copies, remote signals or barrier semaphores. Data moves between devices by JAX's collectives and lax.ppermute only.
A program may use at most 128 MiB of HBM per device.

```python
import math
import jax
import jax.numpy as jnp
from jax import lax

CH = 256
ROUTED = 8
TOP = 4
SHARED = 2
TILE = 16
KH = 64
KW = 32
BANDS = 16
H = 384
W = 128
TR = 24
TC = 8
SLOTS = 6
EXPERTS = 10


def with_ends(array, key, smallest, largest):
    dims = array.shape
    place = [jax.random.randint(jax.random.fold_in(key, axis), (), 0, dims[axis]) for axis in range(len(dims))]
    array = array.at[tuple(place)].set(smallest)
    longest = dims.index(max(dims))
    place[longest] = (place[longest] + 1) % dims[longest]
    return array.at[tuple(place)].set(largest)


def block_levels(stream_key, dims, pieces, low, largest):
    factor_of = 1.0
    for position, blocks in pieces:
        heights = jax.random.uniform(jax.random.fold_in(jax.random.fold_in(stream_key, 6), position), (blocks,), jnp.float32, low / len(pieces), largest / len(pieces))
        factor_of = factor_of * jnp.repeat(jnp.exp(heights), dims[position] // blocks).reshape((-1,) + (1,) * (len(dims) - 1 - position))
    return factor_of


def picks_of(rng, rows, count, top, lift):
    order = jax.random.permutation(jax.random.fold_in(rng, 1), count)
    favour = order
    for power in range(3):
        favour = favour * favour // count
    favour = favour * lift // count
    tickets = jax.random.randint(jax.random.fold_in(rng, 2), (rows, count), 0, 4096) + favour
    fixed_rows = jax.random.permutation(jax.random.fold_in(rng, 3), rows)[jnp.arange(count) % rows]
    tickets = jnp.where(jnp.arange(rows)[:, None] == fixed_rows[None, :], 1 << 14, tickets)
    merit = tickets * count + jnp.arange(count)
    return lax.top_k(merit.astype(jnp.int32), top)[1].astype(jnp.int32)


def scatter_about(rng, shape, deviation, bound, cuts=(), kind=jnp.bfloat16):
    drawn = deviation * jax.random.normal(rng, shape, jnp.float32)
    if cuts:
        drawn = drawn * block_levels(rng, shape, cuts, -0.22, 0.18)
    return jnp.clip(drawn, -bound, bound).astype(kind)


def setup_inputs(seed: int = 0) -> dict:
    splits = jax.random.split(jax.random.key(seed), 8)
    return {
        "saved_mid": scatter_about(splits[0], (H, W, CH), 1.0, 6.0, ((0, 8), (1, 4))),
        "out_grad": scatter_about(splits[1], (H, W, CH), 1.0, 6.0, ((0, 8), (1, 4))),
        "expert_weight": scatter_about(splits[2], (EXPERTS, 9, CH, CH), (9 * CH) ** -0.5, 0.125),
        "routes": picks_of(splits[3], TR * TC, ROUTED, TOP, 8192).reshape((TR, TC, TOP)),
        "gates": jnp.clip(0.5 + 1.0 * jax.random.uniform(splits[4], (TR, TC, SLOTS), jnp.float32) ** block_levels(splits[4], (TR, TC, SLOTS), ((0, 8), (1, 4)), -0.2, 0.2), 0.5, 1.5),
        "band_matrix": scatter_about(splits[5], (BANDS, CH, CH), CH ** -0.5, 0.375),
        "band_ids": with_ends(jax.random.randint(splits[6], (KH, KW), 0, BANDS), jax.random.fold_in(splits[6], 1), 0, BANDS - 1).astype(jnp.int32),
    }


tap_offsets = ((-1, -1), (-1, 0), (-1, 1), (0, -1), (0, 0), (0, 1), (1, -1), (1, 0), (1, 1))

def gelu_slope(values):
    normal_cdf = 0.5 * (1.0 + lax.erf(values * 0.7071067811865476))
    density = jnp.exp(-0.5 * values * values) * 0.3989422804014327
    return normal_cdf + values * density

def angle_table(index, freq, period):
    product = index[:, None] * freq[None, :] % period
    theta = product.astype(jnp.float32) * (2.0 * math.pi / period)
    return (jnp.cos(theta), jnp.sin(theta))

def reference(saved_mid, out_grad, expert_weight, routes, gates, band_matrix, band_ids):
    highest = lax.Precision.HIGHEST
    padded_mid = jnp.pad(saved_mid, ((1, 1), (1, 1), (0, 0)))
    flat_weight = expert_weight.reshape(EXPERTS, 9 * CH, CH)
    zero = jnp.int32(0)

    def one_tile(tile_id):
        tile_row = tile_id // TC
        tile_col = tile_id % TC
        window = lax.dynamic_slice(padded_mid, (tile_row * TILE, tile_col * TILE, zero), (TILE + 2, TILE + 2, CH))
        gradient = lax.dynamic_slice(out_grad, (tile_row * TILE, tile_col * TILE, zero), (TILE, TILE, CH))
        gradient = gradient.reshape(TILE * TILE, CH).astype(jnp.float32)
        patches = jnp.stack([window[1 + row_off:1 + row_off + TILE, 1 + col_off:1 + col_off + TILE] for row_off, col_off in tap_offsets], axis=2)
        patches = patches.reshape(TILE * TILE, 9 * CH).astype(jnp.float32)
        chosen_ids = jnp.concatenate([jnp.arange(SHARED, dtype=jnp.int32), routes[tile_row, tile_col].astype(jnp.int32) + SHARED])
        chosen = jnp.take(flat_weight, chosen_ids, axis=0).astype(jnp.float32)
        preact = jnp.einsum('pk,sko->spo', patches, chosen, precision=highest)
        deltas = (gates[tile_row, tile_col][:, None, None] * gelu_slope(preact) * gradient[None]).astype(jnp.bfloat16)
        tap_tile = jnp.einsum('spo,sko->pk', deltas.astype(jnp.float32), chosen, precision=highest)
        return tap_tile.astype(jnp.bfloat16)
    tap_tiles = lax.map(one_tile, jnp.arange(TR * TC, dtype=jnp.int32))
    tap_field = tap_tiles.reshape(TR, TC, TILE, TILE, 9, CH).transpose(0, 2, 1, 3, 4, 5).reshape(H, W, 9, CH)
    grad_mid = out_grad.astype(jnp.float32)
    for tap_index, (row_off, col_off) in enumerate(tap_offsets):
        shifted = jnp.pad(tap_field[:, :, tap_index, :], ((1, 1), (1, 1), (0, 0)))
        grad_mid = grad_mid + shifted[1 - row_off:1 - row_off + H, 1 - col_off:1 - col_off + W].astype(jnp.float32)
    row_modes = jnp.arange(KH, dtype=jnp.int32)
    row_freq = jnp.where(row_modes < KH // 2, row_modes, H - KH + row_modes).astype(jnp.int32)
    row_cos, row_sin = angle_table(jnp.arange(H, dtype=jnp.int32), row_freq, H)
    col_cos, col_sin = angle_table(jnp.arange(W, dtype=jnp.int32), jnp.arange(KW, dtype=jnp.int32), W)
    half_cos = jnp.einsum('hwc,wn->hnc', grad_mid, col_cos, precision=highest)
    half_sin = jnp.einsum('hwc,wn->hnc', grad_mid, col_sin, precision=highest)
    analysis_scale = 1.0 / math.sqrt(H * W)
    coef_cos = (jnp.einsum('hm,hnc->mnc', row_cos, half_cos, precision=highest) - jnp.einsum('hm,hnc->mnc', row_sin, half_sin, precision=highest)) * analysis_scale
    coef_sin = (jnp.einsum('hm,hnc->mnc', row_sin, half_cos, precision=highest) + jnp.einsum('hm,hnc->mnc', row_cos, half_sin, precision=highest)) * analysis_scale
    coef_cos = coef_cos.astype(jnp.bfloat16).astype(jnp.float32)
    coef_sin = coef_sin.astype(jnp.bfloat16).astype(jnp.float32)
    one_hot = (band_ids[:, :, None] == jnp.arange(BANDS, dtype=jnp.int32)[None, None, :]).astype(jnp.float32)
    bands_f = band_matrix.astype(jnp.float32)
    spec_cos = lax.optimization_barrier(jnp.sum(jnp.einsum('mno,bio->mnbi', coef_cos, bands_f, precision=highest) * one_hot[:, :, :, None], axis=2))
    spec_sin = lax.optimization_barrier(jnp.sum(jnp.einsum('mno,bio->mnbi', coef_sin, bands_f, precision=highest) * one_hot[:, :, :, None], axis=2))
    spec_cos = spec_cos.astype(jnp.bfloat16).astype(jnp.float32)
    spec_sin = spec_sin.astype(jnp.bfloat16).astype(jnp.float32)
    z_cos = jnp.einsum('mnc,hm->hnc', spec_cos, row_cos, precision=highest) + jnp.einsum('mnc,hm->hnc', spec_sin, row_sin, precision=highest)
    z_sin = jnp.einsum('mnc,hm->hnc', spec_sin, row_cos, precision=highest) - jnp.einsum('mnc,hm->hnc', spec_cos, row_sin, precision=highest)
    spectral = jnp.einsum('hnc,wn->hwc', z_cos, col_cos, precision=highest) + jnp.einsum('hnc,wn->hwc', z_sin, col_sin, precision=highest)
    spectral = spectral / math.sqrt(2 * KH * KW)
    return (grad_mid + spectral).astype(jnp.bfloat16)
```

```python
import functools
import math

import jax
import jax.numpy as jnp
from jax import lax
from jax.experimental import pallas as pl
from jax.experimental.pallas import tpu as pltpu
from jax.sharding import PartitionSpec as P

SHARED = 2
TILE = 16
KH = 64
KW = 32
LANES = 128
F32 = jnp.float32
BF16 = jnp.bfloat16
NT = (((1,), (1,)), ((), ()))
VMEM_LIMIT = 44 << 20


def round_up(value, unit):
    return -(-value // unit) * unit


def layout(mesh_rows, cols_dev):
    slots = KH // 2 // mesh_rows
    reals = 2 * slots
    groups = max(1, 16 // reals)
    width = cols_dev + 2
    fold = -(-width // reals)
    unit = 8 * groups // math.gcd(8, groups)
    virtual = round_up(max(width + fold, reals * fold), unit)
    return slots, reals, groups, width, fold, virtual, virtual // groups


def gelu_slope(values):
    size = jnp.abs(values)
    t = 1.0 / (1.0 + 0.23164189 * size)
    bell = jnp.exp(-0.5 * values * values)
    poly = 0.5307027145 * t - 0.7265760135
    poly = poly * t + 0.7107068705
    poly = poly * t - 0.1422483680
    poly = poly * t + 0.1274147960
    tail = bell * (poly * t - 0.3989422804 * size)
    return jnp.where(values >= 0.0, 1.0 - tail, tail)


def get_rows(ref, start, count, stride=None):
    return jnp.concatenate([ref[h, pl.ds(start, count, stride), :] for h in range(ref.shape[0])], axis=1)


def set_rows(ref, start, values, stride=None):
    for h in range(ref.shape[0]):
        ref[h, pl.ds(start, values.shape[0], stride), :] = values[:, h * LANES : (h + 1) * LANES]


def planes(rows, ch):
    return pltpu.VMEM((ch // LANES, rows, LANES), F32)


def conv_kernel(sizes, routes, gates, valid, x, left, right, top, bottom, grad_out, weight, row_table,
                keep, give, grad, e_left, e_right, e_top, e_bottom,
                shifted, patch, delta, acc, ext, sums, lcol, rcol):
    rows_dev, cols_dev, ch = x.shape
    slots, reals, groups, width, fold, virtual, per = sizes
    chips = keep.shape[0]
    across = cols_dev // TILE
    tiles = (rows_dev // TILE) * across
    area = TILE * TILE
    column = lax.broadcasted_iota(jnp.int32, (cols_dev, ch), 0)

    lcol[...] = left[...].astype(F32) * valid[0]
    rcol[...] = right[...].astype(F32) * valid[1]

    def put_row(at, row, low, high):
        shifted[1, at] = row.astype(BF16)
        shifted[0, at] = jnp.where(column == 0, low, pltpu.roll(row, 1, 0)).astype(BF16)
        shifted[2, at] = jnp.where(column == cols_dev - 1, high, pltpu.roll(row, cols_dev - 1, 0)).astype(BF16)

    def fill(step, carry):
        for sub in range(8):
            at = step * 8 + sub
            put_row(at + 1, x[at].astype(F32), lcol[pl.ds(at, 1), :], rcol[pl.ds(at, 1), :])
        return carry

    lax.fori_loop(0, rows_dev // 8, fill, 0)
    for ref, at, flag in ((top, 0, valid[2]), (bottom, rows_dev + 1, valid[3])):
        edge = ref[...].astype(F32) * flag
        put_row(at, edge[:cols_dev], edge[cols_dev : cols_dev + 1], edge[cols_dev + 1 : cols_dev + 2])

    def clear(at, carry):
        for b in range(3):
            acc[b, at] = jnp.zeros((cols_dev, ch), F32)
        return carry

    lax.fori_loop(0, rows_dev + 2, clear, 0)

    def one_tile(tile, carry):
        row = tile // across * TILE
        col = pl.multiple_of(tile % across * TILE, TILE)
        for a in range(3):
            for b in range(3):
                tap = 3 * a + b
                patch[:, tap * ch : (tap + 1) * ch] = shifted[
                    b, pl.ds(row + a, TILE), pl.ds(col, TILE), :
                ].reshape(area, ch)
        upstream = grad_out[pl.ds(row, TILE), pl.ds(col, TILE), :].reshape(area, ch).astype(F32)
        top_count = routes.shape[1]
        experts = list(range(SHARED)) + [routes[tile, k] + SHARED for k in range(top_count)]
        count = len(experts)
        for first in range(0, count, 2):
            pair = range(first, min(first + 2, count))
            kernel = jnp.concatenate([weight[experts[s]] for s in pair], axis=1)
            preact = jnp.dot(patch[...], kernel, preferred_element_type=F32)
            for place, s in enumerate(pair):
                slope = gelu_slope(preact[:, place * ch : (place + 1) * ch])
                delta[:, s * ch : (s + 1) * ch] = (gates[tile, s] * slope * upstream).astype(BF16)
        for a in range(3):
            total = None
            for s in range(count):
                part = lax.dot_general(
                    delta[:, s * ch : (s + 1) * ch],
                    weight[experts[s], a * 3 * ch : (a + 1) * 3 * ch, :],
                    NT,
                    preferred_element_type=F32,
                )
                total = part if total is None else total + part
            for b in range(3):
                acc[b, pl.ds(row + a, TILE), pl.ds(col, TILE), :] += total[:, b * ch : (b + 1) * ch].reshape(
                    TILE, TILE, ch
                )
        return carry

    lax.fori_loop(0, tiles, one_tile, 0)

    filler = jnp.zeros((virtual - cols_dev, ch), F32)

    def put_ext(at, inner):
        middle = acc[1, at] + inner if inner is not None else acc[1, at]
        total = jnp.concatenate([acc[0, at], filler], axis=0)
        total = total + pltpu.roll(jnp.concatenate([middle, filler], axis=0), 1, 0)
        total = total + pltpu.roll(jnp.concatenate([acc[2, at], filler], axis=0), 2, 0)
        set_rows(ext, pl.multiple_of(at * virtual, 8), total)
        return pltpu.roll(total, virtual - 1, 0)[:cols_dev]

    def join(step, carry):
        for sub in range(4):
            at = step * 4 + sub
            grad[at] = put_ext(at + 1, grad_out[at].astype(F32))
        return carry

    lax.fori_loop(0, rows_dev // 4, join, 0)
    e_top[...] = put_ext(0, None).astype(BF16)
    e_bottom[...] = put_ext(rows_dev + 1, None).astype(BF16)
    for ref, at in ((e_left, 0), (e_right, width - 1)):
        ref[:rows_dev] = get_rows(ext, virtual + at, rows_dev, virtual).astype(BF16)
        ref[rows_dev:] = jnp.concatenate(
            [
                get_rows(ext, at, 1),
                get_rows(ext, (rows_dev + 1) * virtual + at, 1),
                jnp.zeros((ref.shape[0] - rows_dev - 2, ch), F32),
            ],
            axis=0,
        ).astype(BF16)

    depth = row_table.shape[1]
    set_rows(ext, (rows_dev + 2) * virtual, jnp.zeros(((depth - rows_dev - 2) * virtual, ch), F32))
    sums[...] = jnp.zeros(sums.shape, F32)
    later = {}

    def emit(v, found):
        for half, ref in enumerate((keep, give)):
            for c in range(chips):
                begin = (half * chips + c) * reals
                parts = []
                for u in range(v, virtual, per):
                    if u < width:
                        parts.append(found[u][begin : begin + reals])
                    elif u < width + fold:
                        parts.append(get_rows(sums, u - width, reals, fold))
                    else:
                        parts.append(jnp.zeros((reals, ch), F32))
                ref[c, :, v * ch : (v + 1) * ch] = jnp.concatenate(parts, axis=0).astype(BF16)

    for v in range(per):
        wanted = [u for u in range(v, virtual, per) if u < width]
        cells = jnp.concatenate(
            [get_rows(ext, u, depth, virtual).astype(BF16) for u in wanted], axis=1
        )
        freqs = jnp.dot(row_table[...], cells, preferred_element_type=F32)
        found = {u: freqs[:, i * ch : (i + 1) * ch] for i, u in enumerate(wanted)}
        at = 2 * chips * reals
        for u in wanted:
            set_rows(sums, u, found[u][at : at + 1])
        if len(wanted) == groups:
            emit(v, found)
        else:
            later[v] = found
    for v, found in later.items():
        emit(v, found)


def regroup_kernel(sizes, parts, out, rows):
    slots, reals, groups, width, fold, virtual, per = sizes
    ch = out.shape[2]
    set_rows(rows, reals * virtual, jnp.zeros((virtual, ch), F32))
    for v in range(per):
        total = parts[0, :, v * ch : (v + 1) * ch].astype(F32)
        for c in range(1, parts.shape[0]):
            total = total + parts[c, :, v * ch : (v + 1) * ch].astype(F32)
        for i, u in enumerate(range(v, virtual, per)):
            piece = total[i * reals : (i + 1) * reals]
            set_rows(rows, u, piece, virtual)
            if width <= u < width + fold:
                set_rows(rows, reals * virtual + u - width, piece, fold)
    for j in range(slots):
        block = [get_rows(rows, 2 * j * virtual, 2 * virtual), get_rows(rows, reals * virtual, virtual)]
        spare = out.shape[1] - 3 * virtual
        if spare:
            block.append(jnp.zeros((spare, ch), F32))
        out[j] = jnp.concatenate(block, axis=0).astype(BF16)


def modes_kernel(virtual, scale, back_scale, first, parts, col_table, back_table, ids, bands, out):
    sources, slots, _, ch = parts.shape
    cols_dev = out.shape[2] // 3
    for s in range(slots):
        special = first[s] > 0
        cosines, sines, plain = [], [], []
        for z in range(sources):
            block = parts[z, s].astype(F32)
            cosines.append(block[:virtual])
            sines.append(block[virtual : 2 * virtual])
            plain.append(block[2 * virtual : 3 * virtual])
        cosine = jnp.concatenate(cosines, axis=0)
        sine = jnp.concatenate(sines, axis=0)
        low_cos = jnp.where(special, jnp.concatenate(plain, axis=0), cosine)
        low_sin = jnp.where(special, 0.0, sine)
        cells = jnp.concatenate([low_cos, low_sin, cosine, sine], axis=1).astype(BF16)
        freqs = jnp.dot(col_table[...], cells, preferred_element_type=F32)
        over_cos, over_sin = freqs[:KW], freqs[KW:]
        coefs = jnp.concatenate(
            [
                over_cos[:, :ch] - over_sin[:, ch : 2 * ch],
                over_cos[:, 2 * ch : 3 * ch] + over_sin[:, 3 * ch :],
                over_cos[:, ch : 2 * ch] + over_sin[:, :ch],
                over_sin[:, 2 * ch : 3 * ch] - over_cos[:, 3 * ch :],
            ],
            axis=0,
        )
        coefs = (coefs * scale).astype(BF16)
        band = ids[s]
        mixed = None
        for b in range(bands.shape[0]):
            chosen = jnp.where(band == b, coefs, jnp.zeros_like(coefs))
            part = lax.dot_general(chosen, bands[b], NT, preferred_element_type=F32)
            mixed = part if mixed is None else mixed + part
        mixed = (mixed * back_scale).astype(BF16)
        plus_cos, minus_cos = mixed[:KW], mixed[KW : 2 * KW]
        plus_sin, minus_sin = mixed[2 * KW : 3 * KW], mixed[3 * KW :]
        sides = jnp.concatenate(
            [
                jnp.concatenate([plus_cos, plus_sin], axis=0),
                jnp.concatenate([plus_sin, -plus_cos], axis=0),
                jnp.concatenate([minus_cos, minus_sin], axis=0),
                jnp.concatenate([-minus_sin, minus_cos], axis=0),
            ],
            axis=1,
        )
        field = jnp.dot(back_table[...], sides, preferred_element_type=F32)
        plus_p, plus_q = field[:, :ch], field[:, ch : 2 * ch]
        both_p = jnp.where(special, 0.0, plus_p) + field[:, 2 * ch : 3 * ch]
        both_q = jnp.where(special, 0.0, plus_q) + field[:, 3 * ch :]
        alone = jnp.where(special, plus_p, 0.0)
        for z in range(sources):
            span = slice(z * cols_dev, (z + 1) * cols_dev)
            out[z, s] = jnp.concatenate([both_p[span], both_q[span], alone[span]], axis=0).astype(BF16)


def final_kernel(valid, mine, theirs, table, grad, left, right, top, bottom, out, rows, cells, lcol, rcol):
    rows_dev, cols_dev, ch = out.shape
    chips, block = mine.shape[:2]
    main = block - cols_dev
    depth = table.shape[1]
    for half, ref in enumerate((mine, theirs)):
        for c in range(chips):
            begin = (half * chips + c) * main
            set_rows(rows, begin, ref[c, :main].astype(F32))
    used = 2 * chips * main
    set_rows(rows, used, mine[0, main:].astype(F32) + theirs[0, main:].astype(F32))
    set_rows(rows, used + cols_dev, jnp.zeros((rows.shape[1] - used - cols_dev, ch), F32))
    lcol[...] = left[:rows_dev].astype(F32) * valid[0]
    rcol[...] = right[:rows_dev].astype(F32) * valid[1]
    for w in range(0, cols_dev, 2):
        modes = jnp.concatenate(
            [get_rows(rows, w + i, depth, cols_dev).astype(BF16) for i in range(2)], axis=1
        )
        lines = jnp.dot(table[...], modes, preferred_element_type=F32)
        for i in range(2):
            set_rows(cells, w + i, lines[:, i * ch : (i + 1) * ch], cols_dev)
    column = lax.broadcasted_iota(jnp.int32, (cols_dev, ch), 0)

    def total(at):
        line = get_rows(cells, pl.multiple_of(at * cols_dev, 8), cols_dev) + grad[at]
        line = line + jnp.where(column == 0, lcol[pl.ds(at, 1), :], 0.0)
        return line + jnp.where(column == cols_dev - 1, rcol[pl.ds(at, 1), :], 0.0)

    def store(step, carry):
        for sub in range(4):
            at = step * 4 + sub
            out[at] = total(at).astype(BF16)
        return carry

    lax.fori_loop(0, rows_dev // 4, store, 0)
    out[0] = (total(0) + top[...].astype(F32) * valid[2]).astype(BF16)
    last = rows_dev - 1
    out[last] = (total(last) + bottom[...].astype(F32) * valid[3]).astype(BF16)


def in_vmem():
    return pl.BlockSpec(memory_space=pltpu.VMEM)


def in_smem():
    return pl.BlockSpec(memory_space=pltpu.SMEM)


def call(kernel, out_shapes, in_specs, scratch, name):
    many = isinstance(out_shapes, (list, tuple))
    return pl.pallas_call(
        kernel,
        out_shape=out_shapes,
        in_specs=in_specs,
        out_specs=[in_vmem() for _ in out_shapes] if many else in_vmem(),
        scratch_shapes=scratch,
        compiler_params=pltpu.CompilerParams(vmem_limit_bytes=VMEM_LIMIT),
        name=name,
    )


def cos_sin(product, period):
    theta = (product % period).astype(F32) * (2.0 * math.pi / period)
    return jnp.cos(theta), jnp.sin(theta)


def body(saved_mid, out_grad, expert_weight, routes, gates, band_matrix, band_ids):
    rows_dev, cols_dev, ch = saved_mid.shape
    n_gx, n_gy = lax.axis_size("gx"), lax.axis_size("gy")
    gx, gy = lax.axis_index("gx"), lax.axis_index("gy")
    full_rows, full_cols = rows_dev * n_gx, cols_dev * n_gy
    sizes = layout(n_gx, cols_dev)
    slots, reals, groups, width, fold, virtual, per = sizes
    chips = n_gx // 2
    core = gx % 2
    same_core = [list(range(start, n_gx, 2)) for start in range(2)]
    swap = [(i, i ^ 1) for i in range(n_gx)]
    experts = expert_weight.shape[0]

    def ring(array, axis, step):
        count = lax.axis_size(axis)
        return lax.ppermute(array, axis, [(i, (i + step) % count) for i in range(count)])

    def shape(*dims, dtype=BF16):
        return jax.ShapeDtypeStruct(dims, dtype)

    valid = jnp.stack([gy > 0, gy < n_gy - 1, gx > 0, gx < n_gx - 1]).astype(F32)

    chip_ids = jnp.arange(chips, dtype=jnp.int32)
    owners = jnp.concatenate([2 * chip_ids + core, 2 * chip_ids + 1 - core])
    slot_ids = (owners[:, None] * slots + jnp.arange(slots, dtype=jnp.int32)[None, :]).reshape(-1)
    freqs = jnp.where(slot_ids == 0, KH // 2, slot_ids)
    used = 2 * chips * reals
    depth_out = round_up(used + 1, 16)

    def row_angles(rows):
        cosine, sine = cos_sin(rows[:, None] * freqs[None, :], full_rows)
        table = jnp.stack([cosine, sine], axis=2).reshape(rows.shape[0], used)
        ones = jnp.ones((rows.shape[0], 1), F32)
        spare = jnp.zeros((rows.shape[0], depth_out - used - 1), F32)
        return jnp.concatenate([table, ones, spare], axis=1)

    depth_in = round_up(rows_dev + 2, 16)
    ext_rows = gx * rows_dev - 1 + jnp.arange(depth_in, dtype=jnp.int32)
    inside = (ext_rows >= 0) & (ext_rows < full_rows) & (jnp.arange(depth_in) < rows_dev + 2)
    row_table = jnp.where(inside[:, None], row_angles(ext_rows), 0.0).T.astype(BF16)
    back_rows = row_angles(gx * rows_dev + jnp.arange(rows_dev, dtype=jnp.int32)).astype(BF16)

    wide = jnp.arange(virtual, dtype=jnp.int32)[None, :]
    ext_cols = jnp.arange(n_gy, dtype=jnp.int32)[:, None] * cols_dev - 1 + wide
    inside = ((ext_cols >= 0) & (ext_cols < full_cols) & (wide < width)).reshape(-1)
    col_modes = jnp.arange(KW, dtype=jnp.int32)
    cosine, sine = cos_sin(col_modes[:, None] * ext_cols.reshape(-1)[None, :], full_cols)
    col_table = jnp.where(inside[None, :], jnp.concatenate([cosine, sine], axis=0), 0.0).astype(BF16)
    cosine, sine = cos_sin(jnp.arange(full_cols, dtype=jnp.int32)[:, None] * col_modes[None, :], full_cols)
    back_cols = jnp.concatenate([cosine, sine], axis=1).astype(BF16)

    left = ring(saved_mid[:, cols_dev - 1, :], "gy", 1)
    right = ring(saved_mid[:, 0, :], "gy", -1)

    def edge_row(at):
        corners = [
            left[at : at + 1] * valid[0].astype(BF16),
            right[at : at + 1] * valid[1].astype(BF16),
        ]
        return jnp.concatenate([saved_mid[at], *corners], axis=0)

    bottom = ring(edge_row(0), "gx", -1)
    top = ring(edge_row(rows_dev - 1), "gx", 1)

    tiles = (rows_dev // TILE) * (cols_dev // TILE)
    packed = per * ch
    edge_rows = rows_dev + 16
    keep, give, grad, e_left, e_right, e_top, e_bottom = call(
        functools.partial(conv_kernel, sizes),
        [
            shape(chips, groups * reals, packed),
            shape(chips, groups * reals, packed),
            shape(rows_dev, cols_dev, ch, dtype=F32),
            shape(edge_rows, ch),
            shape(edge_rows, ch),
            shape(cols_dev, ch),
            shape(cols_dev, ch),
        ],
        [in_smem()] * 3 + [in_vmem()] * 8,
        [
            pltpu.VMEM((3, rows_dev + 2, cols_dev, ch), BF16),
            pltpu.VMEM((TILE * TILE, 9 * ch), BF16),
            pltpu.VMEM((TILE * TILE, (SHARED + routes.shape[2]) * ch), BF16),
            pltpu.VMEM((3, rows_dev + 2, cols_dev, ch), F32),
            planes(depth_in * virtual, ch),
            planes(round_up(max(width, reals * fold), 8), ch),
            pltpu.VMEM((rows_dev, ch), F32),
            pltpu.VMEM((rows_dev, ch), F32),
        ],
        "conv",
    )(
        routes.reshape(tiles, -1),
        gates.reshape(tiles, -1),
        valid,
        saved_mid,
        left,
        right,
        top,
        bottom,
        out_grad,
        expert_weight.reshape(experts, 9 * ch, ch),
        row_table,
    )

    gift = lax.ppermute(give, "gx", swap)
    summed = (keep.astype(F32) + gift.astype(F32)).astype(BF16)
    parts = lax.all_to_all(summed, "gx", 0, 0, tiled=True, axis_index_groups=same_core)
    slot_rows = round_up(3 * virtual, 16)
    regrouped = call(
        functools.partial(regroup_kernel, sizes),
        shape(slots, slot_rows, ch),
        [in_vmem()],
        [planes((reals + 1) * virtual, ch)],
        "regroup",
    )(parts)

    from_left = ring(e_right, "gy", 1)
    from_right = ring(e_left, "gy", -1)

    def with_corners(edge, at):
        low = from_left[at : at + 1].astype(F32) * valid[0]
        high = from_right[at : at + 1].astype(F32) * valid[1]
        column = jnp.arange(cols_dev)[:, None]
        edge = edge.astype(F32) + jnp.where(column == 0, low, 0.0)
        return (edge + jnp.where(column == cols_dev - 1, high, 0.0)).astype(BF16)

    from_below = ring(with_corners(e_top, rows_dev), "gx", -1)
    from_above = ring(with_corners(e_bottom, rows_dev + 1), "gx", 1)

    split = slots % n_gy == 0
    if split:
        here = slots // n_gy
        cells = lax.all_to_all(regrouped.reshape(n_gy, here, slot_rows, ch), "gy", 0, 0, tiled=True)
        first_slot = gx * slots + gy * here
    else:
        here = slots
        cells = lax.all_gather(regrouped, "gy", axis=0)
        first_slot = gx * slots
    my_slots = first_slot + jnp.arange(here, dtype=jnp.int32)
    special = (my_slots == 0).astype(jnp.int32)
    plus_ids = jnp.take(band_ids, my_slots, axis=0)
    minus_ids = jnp.take(band_ids, jnp.where(my_slots == 0, KH // 2, KH - my_slots), axis=0)
    mode_ids = jnp.concatenate([plus_ids, minus_ids, plus_ids, minus_ids], axis=1)[:, :, None]
    mixed = call(
        functools.partial(
            modes_kernel,
            virtual,
            1.0 / math.sqrt(full_rows * full_cols),
            1.0 / math.sqrt(2 * KH * KW),
        ),
        shape(n_gy, here, 3 * cols_dev, ch),
        [in_smem()] + [in_vmem()] * 5,
        [],
        "modes",
    )(special, cells, col_table, back_cols, mode_ids, band_matrix)
    if split:
        mixed = lax.all_to_all(mixed, "gy", 0, 0, tiled=True).reshape(slots, 3 * cols_dev, ch)
    else:
        mixed = lax.dynamic_index_in_dim(mixed, gy, 0, keepdims=False)
    block = jnp.concatenate(
        [mixed[:, : 2 * cols_dev].reshape(slots * 2 * cols_dev, ch), mixed[0, 2 * cols_dev :]], axis=0
    )
    mine = lax.all_gather(block, "gx", axis=0, axis_index_groups=same_core)
    theirs = lax.ppermute(mine, "gx", swap)
    return call(
        final_kernel,
        shape(rows_dev, cols_dev, ch),
        [in_smem()] + [in_vmem()] * 8,
        [
            planes(depth_out * cols_dev, ch),
            planes(rows_dev * cols_dev, ch),
            pltpu.VMEM((rows_dev, ch), F32),
            pltpu.VMEM((rows_dev, ch), F32),
        ],
        "final",
    )(valid, mine, theirs, back_rows, grad, from_left, from_right, from_above, from_below)


def solution(mesh):
    placed = (
        P("gx", "gy", None),
        P("gx", "gy", None),
        P(),
        P("gx", "gy", None),
        P("gx", "gy", None),
        P(),
        P(),
    )
    return jax.shard_map(
        body, mesh=mesh, in_specs=placed, out_specs=P("gx", "gy", None), check_vma=False
    )
```

```python
import functools
import math

import jax
import jax.numpy as jnp
import numpy as np
from jax import lax
from jax.experimental import pallas as pl
from jax.experimental.pallas import tpu as pltpu
from jax.sharding import PartitionSpec as P

SHARED = 2
TILE = 16
KH = 64
KW = 32
LANES = 128
F32 = jnp.float32
BF16 = jnp.bfloat16
NT = (((1,), (1,)), ((), ()))


def round_up(value, unit):
    return -(-value // unit) * unit


def layout(mesh_rows, cols_dev):
    slots = KH // 2 // mesh_rows
    reals = 2 * slots
    groups = max(1, 16 // reals)
    width = cols_dev + 2
    fold = -(-width // reals)
    unit = 8 * groups // math.gcd(8, groups)
    virtual = round_up(max(width + fold, reals * fold), unit)
    return slots, reals, groups, width, fold, virtual, virtual // groups


def gelu_slope(values):
    size = jnp.abs(values)
    t = 1.0 / (1.0 + 0.23164189 * size)
    bell = jnp.exp(-0.5 * values * values)
    poly = 0.5307027145 * t - 0.7265760135
    poly = poly * t + 0.7107068705
    poly = poly * t - 0.1422483680
    poly = poly * t + 0.1274147960
    tail = bell * (poly * t - 0.3989422804 * size)
    return jnp.where(values >= 0.0, 1.0 - tail, tail)


def get_rows(ref, start, count, stride=None):
    return jnp.concatenate([ref[h, pl.ds(start, count, stride), :] for h in range(ref.shape[0])], axis=1)


def set_rows(ref, start, values, stride=None):
    for h in range(ref.shape[0]):
        ref[h, pl.ds(start, values.shape[0], stride), :] = values[:, h * LANES : (h + 1) * LANES]


def planes(rows, ch):
    return pltpu.VMEM((ch // LANES, rows, LANES), F32)


def conv_kernel(sizes, picked, edges, span, routes, gates, place_ref, x_far, left, right, top, bottom, grad_out_far, weight_far, tables,
                keep, give, grad_far, e_left, e_right,
                x, grad_out, weight, grad, shifted, patch, delta_a, delta_b, acc, ext, sums, lcol, rcol,
                weight_sems, field_sems):
    rows_dev, cols_dev, ch = x.shape
    experts = weight.shape[0]
    field_copies = [
        pltpu.make_async_copy(x_far, x, field_sems.at[0]),
        pltpu.make_async_copy(grad_out_far, grad_out, field_sems.at[1]),
        pltpu.make_async_copy(grad, grad_far, field_sems.at[2]),
    ]

    def fetch(e):
        return pltpu.make_async_copy(weight_far.at[e], weight.at[e], weight_sems.at[e])

    def in_first(e):
        found = routes[0] == e - SHARED
        for k in range(1, picked):
            found = found | (routes[k] == e - SHARED)
        return found

    count = SHARED + picked
    early = list(range(SHARED)) + [routes[k] + SHARED for k in range(picked)]
    field_copies[0].start()
    for e in early[:2]:
        fetch(e).start()
    field_copies[1].start()

    slots, reals, groups, width, fold, virtual, per = sizes
    chips = keep.shape[0]
    across = cols_dev // TILE
    tiles = (rows_dev // TILE) * across
    area = TILE * TILE
    column = lax.broadcasted_iota(jnp.int32, (cols_dev, ch), 0)

    valid = neighbours(place_ref, edges)
    lcol[...] = left[...].astype(F32) * valid[0]
    rcol[...] = right[...].astype(F32) * valid[1]
    field_copies[0].wait()
    for e in early[2:4]:
        fetch(e).start()

    def put_row(at, row, low, high):
        shifted[1, at] = row.astype(BF16)
        shifted[0, at] = jnp.where(column == 0, low, pltpu.roll(row, 1, 0)).astype(BF16)
        shifted[2, at] = jnp.where(column == cols_dev - 1, high, pltpu.roll(row, cols_dev - 1, 0)).astype(BF16)

    def fill(step, carry):
        for sub in range(8):
            at = step * 8 + sub
            put_row(at + 1, x[at].astype(F32), lcol[pl.ds(at, 1), :], rcol[pl.ds(at, 1), :])
        return carry

    lax.fori_loop(0, rows_dev // 8, fill, 0)
    for ref, at, flag in ((top, 0, valid[2]), (bottom, rows_dev + 1, valid[3])):
        edge = ref[...].astype(F32) * flag
        low = edge[cols_dev : cols_dev + 1] * valid[0]
        high = edge[cols_dev + 1 : cols_dev + 2] * valid[1]
        put_row(at, edge[:cols_dev], low, high)

    def clear(at, carry):
        for b in range(3):
            acc[b, at] = jnp.zeros((cols_dev, ch), F32)
        return carry

    lax.fori_loop(0, rows_dev + 2, clear, 0)

    firsts = range(0, count, 2)

    def place(tile):
        return tile // across * TILE, pl.multiple_of(tile % across * TILE, TILE)

    def expert(tile, s):
        return s if s < SHARED else routes[tile * picked + s - SHARED] + SHARED

    def gather(tile):
        row, col = place(tile)
        for a in range(3):
            for b in range(3):
                tap = 3 * a + b
                patch[:, tap * ch : (tap + 1) * ch] = shifted[
                    b, pl.ds(row + a, TILE), pl.ds(col, TILE), :
                ].reshape(area, ch)

    def forward(tile, first):
        pair = range(first, min(first + 2, count))
        kernel = jnp.concatenate([weight[expert(tile, s)] for s in pair], axis=1)
        return jnp.dot(patch[...], kernel, preferred_element_type=F32)

    def slopes(tile, first, preact, delta):
        row, col = place(tile)
        upstream = grad_out[pl.ds(row, TILE), pl.ds(col, TILE), :].reshape(area, ch).astype(F32)
        for i, s in enumerate(range(first, min(first + 2, count))):
            slope = gelu_slope(preact[:, i * ch : (i + 1) * ch])
            delta[:, s * ch : (s + 1) * ch] = (gates[tile * count + s] * slope * upstream).astype(BF16)

    def backward(tile, a, delta):
        row, col = place(tile)
        total = None
        for s in range(count):
            part = lax.dot_general(
                delta[:, s * ch : (s + 1) * ch],
                weight[expert(tile, s), a * 3 * ch : (a + 1) * 3 * ch, :],
                NT,
                preferred_element_type=F32,
            )
            total = part if total is None else total + part
        for b in range(3):
            acc[b, pl.ds(row + a, TILE), pl.ds(col, TILE), :] += total[:, b * ch : (b + 1) * ch].reshape(
                TILE, TILE, ch
            )

    def step(tile, source, target):
        gather(tile + 1)
        for i, first in enumerate(firsts):
            preact = forward(tile + 1, first)
            for a in range(i, 3 if first == firsts[-1] else i + 1):
                backward(tile, a, source)
            slopes(tile + 1, first, preact, target)

    gather(0)
    for first in firsts:
        for e in early[first : first + 2]:
            fetch(e).wait()
        for e in early[first + 4 : first + 6]:
            fetch(e).start()
        if first == firsts[-1]:
            for e in range(SHARED, experts):

                @pl.when(jnp.logical_not(in_first(e)))
                def _():
                    fetch(e).start()

        preact = forward(0, first)
        if first == 0:
            field_copies[1].wait()
        slopes(0, first, preact, delta_a)
    for e in range(SHARED, experts):

        @pl.when(jnp.logical_not(in_first(e)))
        def _():
            fetch(e).wait()

    pairs = (tiles - 1) // 2

    def two(i, carry):
        step(2 * i, delta_a, delta_b)
        step(2 * i + 1, delta_b, delta_a)
        return carry

    lax.fori_loop(0, pairs, two, 0)
    last, source = 2 * pairs, delta_a
    if last < tiles - 1:
        step(last, delta_a, delta_b)
        last, source = last + 1, delta_b
    for a in range(3):
        backward(last, a, source)

    filler = jnp.zeros((virtual - cols_dev, ch), F32)

    def put_ext(at, inner):
        middle = acc[1, at] + inner if inner is not None else acc[1, at]
        total = jnp.concatenate([acc[0, at], filler], axis=0)
        total = total + pltpu.roll(jnp.concatenate([middle, filler], axis=0), 1, 0)
        total = total + pltpu.roll(jnp.concatenate([acc[2, at], filler], axis=0), 2, 0)
        set_rows(ext, pl.multiple_of(at * virtual, 8), total)
        return pltpu.roll(total, virtual - 1, 0)[:cols_dev]

    def join(step, carry):
        for sub in range(4):
            at = step * 4 + sub
            grad[at] = put_ext(at + 1, grad_out[at].astype(F32))
        return carry

    lax.fori_loop(0, rows_dev // 4, join, 0)
    field_copies[2].start()
    blocks = []
    for at in (0, rows_dev + 1):
        line = put_ext(at, None)
        corners = [get_rows(ext, at * virtual, 1), get_rows(ext, at * virtual + width - 1, 1)]
        line = jnp.concatenate([line, *corners, jnp.zeros((TILE - 2, ch), F32)], axis=0).astype(BF16)
        blocks += [line[i : i + TILE] for i in range(0, line.shape[0], TILE)]
    for i, block in enumerate(blocks):
        begin = (per + i // chips) * ch
        give[i % chips, :, begin : begin + ch] = block
    for ref, at in ((e_left, 0), (e_right, width - 1)):
        ref[...] = get_rows(ext, virtual + at, rows_dev, virtual).astype(BF16)

    row_table = tables[span]
    depth = row_table.shape[1]
    set_rows(ext, (rows_dev + 2) * virtual, jnp.zeros(((depth - rows_dev - 2) * virtual, ch), F32))
    sums[...] = jnp.zeros(sums.shape, F32)
    later = {}

    def emit(v, found):
        for half, ref in enumerate((keep, give)):
            for c in range(chips):
                begin = (half * chips + c) * reals
                parts = []
                for u in range(v, virtual, per):
                    if u < width:
                        parts.append(found[u][begin : begin + reals])
                    elif u < width + fold:
                        parts.append(get_rows(sums, u - width, reals, fold))
                    else:
                        parts.append(jnp.zeros((reals, ch), F32))
                ref[c, :, v * ch : (v + 1) * ch] = jnp.concatenate(parts, axis=0).astype(BF16)

    for v in range(per):
        wanted = [u for u in range(v, virtual, per) if u < width]
        cells = jnp.concatenate(
            [get_rows(ext, u, depth, virtual).astype(BF16) for u in wanted], axis=1
        )
        freqs = jnp.dot(row_table, cells, preferred_element_type=F32)
        found = {u: freqs[:, i * ch : (i + 1) * ch] for i, u in enumerate(wanted)}
        at = 2 * chips * reals
        for u in wanted:
            set_rows(sums, u, found[u][at : at + 1])
        if len(wanted) == groups:
            emit(v, found)
        else:
            later[v] = found
    for v, found in later.items():
        emit(v, found)
    field_copies[2].wait()


def neighbours(place, edges):
    gx, gy = place[0], place[1]
    found = (gy > 0, gy < edges[1] - 1, gx > 0, gx < edges[0] - 1)
    return [jnp.where(flag, 1.0, 0.0) for flag in found]


def edge_blocks(cols_dev):
    return cols_dev // TILE + 1


def find_edge(gift, chips, per, ch, blocks, which):
    parts = []
    for i in range(which * blocks, (which + 1) * blocks):
        begin = (per + i // chips) * ch
        parts.append(gift[i % chips, :, begin : begin + ch])
    return jnp.concatenate(parts, axis=1)


def regroup_kernel(sizes, chips, here, edges, span, place, gift, e_left, e_right, tables, *refs):
    slots, reals, groups, width, fold, virtual, per = sizes
    parts, (above, below, *outs, rows) = refs[:chips], refs[chips:]
    cols_dev, ch = above.shape
    rows_dev = e_left.shape[0]
    blocks = edge_blocks(cols_dev)
    set_rows(rows, reals * virtual, jnp.zeros((virtual, ch), F32))
    for v in range(per):
        total = None
        for part in parts:
            piece = part[:, v * ch : (v + 1) * ch].astype(F32)
            total = piece if total is None else total + piece
        for i, u in enumerate(range(v, virtual, per)):
            piece = total[i * reals : (i + 1) * reals]
            set_rows(rows, u, piece, virtual)
            if width <= u < width + fold:
                set_rows(rows, reals * virtual + u - width, piece, fold)
    plain = get_rows(rows, reals * virtual, virtual).astype(BF16)
    low = jnp.dot(tables[span], plain, preferred_element_type=F32)
    share = low.shape[0] // 4
    for real in range(reals):
        part = real % 2 * share
        set_rows(rows, real * virtual + width, low[part : part + share])

    valid = neighbours(place, edges)
    first_core = place[0] % 2 == 0

    def line(far, near, flag):
        flat = jnp.where(first_core, far.astype(F32), near.astype(F32)) * flag
        return [flat[:, i * ch : (i + 1) * ch] for i in range(blocks)]

    far_bottom = parts[1][:, per * ch : (per + blocks) * ch]
    far_top = parts[chips - 1][:, per * ch : (per + blocks) * ch]
    from_above = line(far_bottom, find_edge(gift, chips, per, ch, blocks, 1), valid[2])
    from_below = line(find_edge(gift, chips, per, ch, blocks, 0), far_top, valid[3])
    above[...] = jnp.concatenate(from_above[:-1], axis=0).astype(BF16)
    below[...] = jnp.concatenate(from_below[:-1], axis=0).astype(BF16)
    row = lax.broadcasted_iota(jnp.int32, (rows_dev, ch), 0)
    sides = []
    for ref, at in ((e_right, 1), (e_left, 0)):
        side = ref[...].astype(F32)
        side = side + jnp.where(row == 0, from_above[-1][at : at + 1], 0.0)
        sides.append(side + jnp.where(row == rows_dev - 1, from_below[-1][at : at + 1], 0.0))

    for place in range(slots // here):
        block = [get_rows(rows, 2 * place * here * virtual, 2 * here * virtual)]
        if outs[place].shape[0] > block[0].shape[0]:
            block.append(sides[0] if place == 1 else sides[1])
        outs[place][...] = jnp.concatenate(block, axis=0).astype(BF16)
    if here == slots:
        for ref, side in zip(outs[1:], sides):
            ref[...] = side.astype(BF16)


def modes_kernel(sizes, split, scale, back_scale, sources, place, col_table, back_table, ids, bands, *refs):
    slots, reals, groups, width, fold, virtual, per = sizes
    parts, (low_out, *outs) = refs[:sources], refs[sources:]
    ch = low_out.shape[1]
    share = low_out.shape[0] // 4
    here = parts[0].shape[0] // (2 * virtual)
    cols_dev = outs[0].shape[0] // (2 * here)
    first = place[0] * slots + (place[1] * here if split else 0)

    def bands_of(row, rows, begin):
        line = jnp.broadcast_to(ids[pl.ds(row, 1), :], (rows, KW))
        wanted = lax.broadcasted_iota(jnp.int32, (rows, KW), 0) % KW + begin
        at = lax.broadcasted_iota(jnp.int32, (rows, KW), 1)
        return jnp.sum(jnp.where(wanted == at, line, 0).astype(F32), axis=1, keepdims=True)

    low_line = bands_of(0, share, place[0] * share)
    for s in range(here):
        blocks = [part[2 * s * virtual : 2 * (s + 1) * virtual].astype(F32) for part in parts]
        cosine = jnp.concatenate([block[:virtual] for block in blocks], axis=0)
        sine = jnp.concatenate([block[virtual:] for block in blocks], axis=0)
        cells = jnp.concatenate([cosine, sine], axis=1).astype(BF16)
        freqs = jnp.dot(col_table[...], cells, preferred_element_type=F32)
        over_cos, over_sin = freqs[:KW], freqs[KW:]
        slot = first + s
        plus = jnp.where(slot == 0, 0.0, scale)
        low = sum(blocks)
        coefs = jnp.concatenate(
            [
                (over_cos[:, :ch] - over_sin[:, ch:]) * plus,
                (over_cos[:, :ch] + over_sin[:, ch:]) * scale,
                (over_cos[:, ch:] + over_sin[:, :ch]) * plus,
                (over_sin[:, :ch] - over_cos[:, ch:]) * scale,
                low[width : width + share] * scale,
                low[virtual + width : virtual + width + share] * scale,
                jnp.zeros((2 * share, ch), F32),
            ],
            axis=0,
        ).astype(BF16)
        plus_line = bands_of(slot, KW, 0)
        minus_line = bands_of(jnp.where(slot == 0, KH // 2, KH - slot), KW, 0)
        band = jnp.concatenate([plus_line, minus_line, plus_line, minus_line] + [low_line] * 4, axis=0)
        mixed = None
        for b in range(bands.shape[0]):
            chosen = jnp.where(band == float(b), coefs, jnp.zeros_like(coefs))
            part = lax.dot_general(chosen, bands[b], NT, preferred_element_type=F32)
            mixed = part if mixed is None else mixed + part
        mixed = (mixed * back_scale).astype(BF16)
        if s == 0:
            low_out[...] = mixed[4 * KW :]
        plus_cos, minus_cos = mixed[:KW], mixed[KW : 2 * KW]
        plus_sin, minus_sin = mixed[2 * KW : 3 * KW], mixed[3 * KW : 4 * KW]
        sides = jnp.concatenate(
            [
                jnp.concatenate([plus_cos, plus_sin, minus_cos, minus_sin], axis=0),
                jnp.concatenate([plus_sin, -plus_cos, -minus_sin, minus_cos], axis=0),
            ],
            axis=1,
        )
        field = jnp.dot(back_table[...], sides, preferred_element_type=F32).astype(BF16)
        for z, out in enumerate(outs):
            span = slice(z * cols_dev, (z + 1) * cols_dev)
            begin = 2 * s * cols_dev
            out[begin : begin + cols_dev] = field[span, :ch]
            out[begin + cols_dev : begin + 2 * cols_dev] = field[span, ch:]


def final_kernel(count, main, edges, spans, place, tables, grad_far, left, right, above, below, *refs):
    blocks, (out, grad, rows, cells, lcol, rcol, sem) = refs[:count], refs[count:]
    rows_dev, cols_dev, ch = out.shape
    table, low_table = tables[spans[0]], tables[spans[1]]
    depth = table.shape[1]
    valid = neighbours(place, edges)
    grad_copy = pltpu.make_async_copy(grad_far, grad, sem)
    grad_copy.start()
    for place, block in enumerate(blocks):
        set_rows(rows, place * main, block[:main].astype(F32))
    used = count * main
    low = jnp.concatenate([block[main:] for block in blocks], axis=0)
    set_rows(rows, used, jnp.dot(low_table, low, preferred_element_type=F32))
    set_rows(rows, used + cols_dev, jnp.zeros((rows.shape[1] - used - cols_dev, ch), F32))
    lcol[...] = left[left.shape[0] - rows_dev :].astype(F32) * valid[0]
    rcol[...] = right[right.shape[0] - rows_dev :].astype(F32) * valid[1]
    for w in range(0, cols_dev, 2):
        modes = jnp.concatenate(
            [get_rows(rows, w + i, depth, cols_dev).astype(BF16) for i in range(2)], axis=1
        )
        lines = jnp.dot(table, modes, preferred_element_type=F32)
        for i in range(2):
            set_rows(cells, w + i, lines[:, i * ch : (i + 1) * ch], cols_dev)
    column = lax.broadcasted_iota(jnp.int32, (cols_dev, ch), 0)

    def total(at):
        line = get_rows(cells, pl.multiple_of(at * cols_dev, 8), cols_dev) + grad[at]
        line = line + jnp.where(column == 0, lcol[pl.ds(at, 1), :], 0.0)
        return line + jnp.where(column == cols_dev - 1, rcol[pl.ds(at, 1), :], 0.0)

    grad_copy.wait()

    def store(step, carry):
        for sub in range(4):
            at = step * 4 + sub
            out[at] = total(at).astype(BF16)
        return carry

    lax.fori_loop(0, rows_dev // 4, store, 0)
    out[0] = (total(0) + above[...].astype(F32)).astype(BF16)
    last = rows_dev - 1
    out[last] = (total(last) + below[...].astype(F32)).astype(BF16)


def in_vmem():
    return pl.BlockSpec(memory_space=pltpu.VMEM)


def in_hbm():
    return pl.BlockSpec(memory_space=pltpu.HBM)


def in_smem():
    return pl.BlockSpec(memory_space=pltpu.SMEM)


def call(kernel, out_shapes, in_specs, scratch, name, limit, out_specs=None):
    many = isinstance(out_shapes, (list, tuple))
    return pl.pallas_call(
        kernel,
        out_shape=out_shapes,
        in_specs=in_specs,
        out_specs=out_specs or ([in_vmem() for _ in out_shapes] if many else in_vmem()),
        scratch_shapes=scratch,
        compiler_params=pltpu.CompilerParams(vmem_limit_bytes=limit << 20),
        name=name,
    )


def cos_sin(product, period):
    theta = (product % period) * (2.0 * math.pi / period)
    return np.cos(theta), np.sin(theta)


def padded(table, rows, cols):
    return np.pad(table, ((0, rows - table.shape[0]), (0, cols - table.shape[1])))


def angle_tables(n_gx, n_gy, rows_dev, cols_dev):
    sizes = layout(n_gx, cols_dev)
    slots, reals, groups, width, fold, virtual, per = sizes
    chips, share = n_gx // 2, KW // n_gx
    split = slots % n_gy == 0
    here = slots // n_gy if split else slots
    full_rows, full_cols = rows_dev * n_gx, cols_dev * n_gy
    used = 2 * chips * reals
    depth_in, depth_out = round_up(rows_dev + 2, 16), round_up(used + 1, 16)
    modes = np.arange(KW)
    chip_ids = np.arange(chips)

    def row_angles(rows, freqs):
        cosine, sine = cos_sin(rows[:, None] * freqs[None, :], full_rows)
        table = np.stack([cosine, sine], axis=2).reshape(len(rows), used)
        ones = np.ones((len(rows), 1))
        return np.concatenate([table, ones, np.zeros((len(rows), depth_out - used - 1))], axis=1)

    def low_angles(cols, owners):
        product = (owners[:, None] * share + np.arange(share)[None, :])[None] * cols[:, None, None]
        cosine, sine = cos_sin(product, full_cols)
        spare = np.zeros_like(cosine)
        return np.concatenate([cosine, sine, spare, spare], axis=2)

    def owners_of(order, core):
        return np.concatenate([2 * order + core, 2 * order + 1 - core])

    both, forth, back = [], [], []
    wide = np.arange(virtual)
    for gy in range(n_gy):
        sources = (gy - np.arange(n_gy)) % n_gy if split else np.arange(n_gy)
        ext_cols = sources[:, None] * cols_dev - 1 + wide[None, :]
        inside = (ext_cols >= 0) & (ext_cols < full_cols) & (wide < width)[None, :]
        cosine, sine = cos_sin(modes[:, None] * ext_cols.reshape(1, -1), full_cols)
        forth.append(np.concatenate([cosine, sine]) * inside.reshape(1, -1))
        all_cols = (sources[:, None] * cols_dev + np.arange(cols_dev)[None, :]).reshape(-1, 1)
        back.append(np.concatenate(cos_sin(all_cols * modes[None, :], full_cols) * 2, axis=1))
    for gx in range(n_gx):
        chip, core = gx // 2, gx % 2
        for gy in range(n_gy):
            places = np.arange(slots)
            if split:
                places = (places + gy * here) % slots

            def frequencies(owners):
                ids = (owners[:, None] * slots + places[None, :]).reshape(-1)
                return np.where(ids == 0, KH // 2, ids)

            order = (chip_ids + chip) % chips
            ext_rows = gx * rows_dev - 1 + np.arange(depth_in)
            inside = (ext_rows >= 0) & (ext_rows < full_rows) & (np.arange(depth_in) < rows_dev + 2)
            row_table = (row_angles(ext_rows, frequencies(owners_of(order, core))) * inside[:, None]).T
            owners = owners_of((chip - chip_ids) % chips, core)
            back_rows = row_angles(gx * rows_dev + np.arange(rows_dev), frequencies(owners))
            cols = gy * cols_dev - 1 + wide
            inside = (cols >= 0) & (cols < full_cols) & (wide < width)
            low_table = (low_angles(cols, np.array([gx]))[:, 0] * inside[:, None]).T
            back_low = low_angles(gy * cols_dev + np.arange(cols_dev), owners).reshape(cols_dev, -1)
            tables = [row_table, back_rows, low_table, back_low]
            lanes = round_up(max(table.shape[1] for table in tables), LANES)
            both.append(np.concatenate([padded(t, round_up(len(t), 16), lanes) for t in tables]))
    both = np.stack(both).reshape(n_gx, n_gy, *both[0].shape)
    return [np.asarray(table, np.float32).astype(BF16) for table in (both, np.stack(forth), np.stack(back))]


def table_spans(sizes, rows_dev, cols_dev, n_gx):
    slots, reals, groups, width, fold, virtual, per = sizes
    used, share = n_gx * reals, KW // n_gx
    shapes = [
        (round_up(used + 1, 16), round_up(rows_dev + 2, 16)),
        (rows_dev, round_up(used + 1, 16)),
        (4 * share, virtual),
        (cols_dev, n_gx * 4 * share),
    ]
    spans, begin = [], 0
    for rows, cols in shapes:
        spans.append((slice(begin, begin + rows), slice(0, cols)))
        begin += round_up(rows, 16)
    return spans


def body(saved_mid, out_grad, expert_weight, routes, gates, band_matrix, band_ids):
    rows_dev, cols_dev, ch = saved_mid.shape
    n_gx, n_gy = lax.axis_size("gx"), lax.axis_size("gy")
    gx, gy = lax.axis_index("gx"), lax.axis_index("gy")
    full_rows, full_cols = rows_dev * n_gx, cols_dev * n_gy
    sizes = layout(n_gx, cols_dev)
    slots, reals, groups, width, fold, virtual, per = sizes
    chips = n_gx // 2
    swap = [(i, i ^ 1) for i in range(n_gx)]
    experts = expert_weight.shape[0]

    def ring(array, axis, step):
        count = lax.axis_size(axis)
        return lax.ppermute(array, axis, [(i, (i + step) % count) for i in range(count)])

    def shape(*dims, dtype=BF16):
        return jax.ShapeDtypeStruct(dims, dtype)

    split = slots % n_gy == 0
    here = slots // n_gy if split else slots
    depth_in, depth_out = round_up(rows_dev + 2, 16), round_up(n_gx * reals + 1, 16)
    spans = table_spans(sizes, rows_dev, cols_dev, n_gx)
    tables, col_tables, back_tables = angle_tables(n_gx, n_gy, rows_dev, cols_dev)
    tables = jnp.asarray(tables)[gx, gy]
    col_table, back_table = jnp.asarray(col_tables)[gy], jnp.asarray(back_tables)[gy]
    share = KW // n_gx
    place = jnp.stack([gx, gy]).astype(jnp.int32)
    edges = (n_gx, n_gy)

    left = ring(saved_mid[:, cols_dev - 1, :], "gy", 1)
    right = ring(saved_mid[:, 0, :], "gy", -1)

    def edge_row(at):
        return jnp.concatenate([saved_mid[at], left[at : at + 1], right[at : at + 1]], axis=0)

    bottom = ring(edge_row(0), "gx", -1)
    top = ring(edge_row(rows_dev - 1), "gx", 1)

    picked = routes.shape[2]
    packed = per * ch
    lines = edge_blocks(cols_dev)
    extra = -(-2 * lines // chips) * ch
    keep, give, grad, e_left, e_right = call(
        functools.partial(conv_kernel, sizes, picked, edges, spans[0]),
        [
            shape(chips, groups * reals, packed),
            shape(chips, groups * reals, packed + extra),
            pltpu.HBM((rows_dev, cols_dev, ch), F32),
            shape(rows_dev, ch),
            shape(rows_dev, ch),
        ],
        [in_smem()] * 3 + [in_hbm()] + [in_vmem()] * 4 + [in_hbm()] * 2 + [in_vmem()],
        [
            pltpu.VMEM((rows_dev, cols_dev, ch), BF16),
            pltpu.VMEM((rows_dev, cols_dev, ch), BF16),
            pltpu.VMEM((experts, 9 * ch, ch), BF16),
            pltpu.VMEM((rows_dev, cols_dev, ch), F32),
            pltpu.VMEM((3, rows_dev + 2, cols_dev, ch), BF16),
            pltpu.VMEM((TILE * TILE, 9 * ch), BF16),
            pltpu.VMEM((TILE * TILE, (SHARED + picked) * ch), BF16),
            pltpu.VMEM((TILE * TILE, (SHARED + picked) * ch), BF16),
            pltpu.VMEM((3, rows_dev + 2, cols_dev, ch), F32),
            planes(depth_in * virtual, ch),
            planes(round_up(max(width, reals * fold), 8), ch),
            pltpu.VMEM((rows_dev, ch), F32),
            pltpu.VMEM((rows_dev, ch), F32),
            pltpu.SemaphoreType.DMA((experts,)),
            pltpu.SemaphoreType.DMA((3,)),
        ],
        "conv",
        40,
        [in_vmem()] * 2 + [in_hbm()] + [in_vmem()] * 2,
    )(
        routes.reshape(-1),
        gates.reshape(-1),
        place,
        pltpu.with_memory_space_constraint(saved_mid, pltpu.HBM),
        left,
        right,
        top,
        bottom,
        pltpu.with_memory_space_constraint(out_grad, pltpu.HBM),
        pltpu.with_memory_space_constraint(expert_weight.reshape(experts, 9 * ch, ch), pltpu.HBM),
        tables,
    )

    gift = lax.ppermute(give, "gx", swap)
    messages = [(keep[d].astype(F32) + gift[d, :, :packed].astype(F32)).astype(BF16) for d in range(chips)]
    for d, which in ((1, 1), (chips - 1, 0)):
        edge = find_edge(gift, chips, per, ch, lines, which)
        messages[d] = jnp.concatenate([messages[d], edge], axis=1)
    parts = [messages[0]] + [ring(messages[d], "gx", 2 * d) for d in range(1, chips)]
    block_rows = here * 2 * virtual
    if split:
        ends = [rows_dev if d in (1, n_gy - 1) else 0 for d in range(n_gy)]
        regrouped = [shape(block_rows + end, ch) for end in ends]
    else:
        regrouped = [shape(block_rows, ch), shape(rows_dev, ch), shape(rows_dev, ch)]
    from_above, from_below, *regrouped = call(
        functools.partial(regroup_kernel, sizes, chips, here, edges, spans[2]),
        [shape(cols_dev, ch), shape(cols_dev, ch), *regrouped],
        [in_smem()] + [in_vmem()] * (4 + chips),
        [planes((reals + 1) * virtual, ch)],
        "regroup",
        8,
    )(place, gift, e_left, e_right, tables, *parts)

    if split:
        cells = [regrouped[0]] + [ring(regrouped[d], "gy", d) for d in range(1, n_gy)]
        from_left, from_right = cells[1], cells[n_gy - 1]
    else:
        gathered = lax.all_gather(regrouped[0], "gy", axis=0)
        cells = [gathered[z] for z in range(n_gy)]
        from_left, from_right = ring(regrouped[1], "gy", 1), ring(regrouped[2], "gy", -1)
    low_modes, *mixed = call(
        functools.partial(
            modes_kernel,
            sizes,
            split,
            1.0 / math.sqrt(full_rows * full_cols),
            1.0 / math.sqrt(2 * KH * KW),
            n_gy,
        ),
        [shape(4 * share, ch)] + [shape(here * 2 * cols_dev, ch) for _ in range(n_gy)],
        [in_smem()] + [in_vmem()] * (4 + n_gy),
        [],
        "modes",
        12,
    )(place, col_table, back_table, band_ids, band_matrix, *cells)
    if split:
        mixed = [mixed[0]] + [ring(mixed[d], "gy", -d) for d in range(1, n_gy)]
    else:
        mixed = [lax.dynamic_index_in_dim(jnp.stack(mixed), gy, 0, keepdims=False)]
    block = jnp.concatenate([*mixed, low_modes], axis=0)

    blocks = [block] + [ring(block, "gx", 2 * d) for d in range(1, chips)]
    blocks = blocks + [lax.ppermute(array, "gx", swap) for array in blocks]
    return call(
        functools.partial(final_kernel, n_gx, slots * 2 * cols_dev, edges, (spans[1], spans[3])),
        shape(rows_dev, cols_dev, ch),
        [in_smem(), in_vmem(), in_hbm()] + [in_vmem()] * (4 + n_gx),
        [
            pltpu.VMEM((rows_dev, cols_dev, ch), F32),
            planes(depth_out * cols_dev, ch),
            planes(rows_dev * cols_dev, ch),
            pltpu.VMEM((rows_dev, ch), F32),
            pltpu.VMEM((rows_dev, ch), F32),
            pltpu.SemaphoreType.DMA,
        ],
        "final",
        16,
    )(place, tables, grad, from_left, from_right, from_above, from_below, *blocks)


def solution(mesh):
    placed = (
        P("gx", "gy", None),
        P("gx", "gy", None),
        P(),
        P("gx", "gy", None),
        P("gx", "gy", None),
        P(),
        P(),
    )
    return jax.shard_map(
        body, mesh=mesh, in_specs=placed, out_specs=P("gx", "gy", None), check_vma=False
    )
```

```python
import functools
import math

import jax
import jax.numpy as jnp
import numpy as np
from jax import lax
from jax.experimental import pallas as pl
from jax.experimental.pallas import tpu as pltpu
from jax.sharding import PartitionSpec as P

SHARED = 2
TILE = 16
KH = 64
KW = 32
LANES = 128
F32 = jnp.float32
BF16 = jnp.bfloat16
NT = (((1,), (1,)), ((), ()))


def round_up(value, unit):
    return -(-value // unit) * unit


def layout(mesh_rows, cols_dev):
    slots = KH // 2 // mesh_rows
    reals = 2 * slots
    groups = max(1, 16 // reals)
    width = cols_dev + 2
    fold = -(-width // reals)
    unit = 8 * groups // math.gcd(8, groups)
    virtual = round_up(max(width + fold, reals * fold), unit)
    return slots, reals, groups, width, fold, virtual, virtual // groups


def gelu_slope(values):
    size = jnp.abs(values)
    t = 1.0 / (1.0 + 0.23164189 * size)
    bell = jnp.exp(-0.5 * values * values)
    poly = 0.5307027145 * t - 0.7265760135
    poly = poly * t + 0.7107068705
    poly = poly * t - 0.1422483680
    poly = poly * t + 0.1274147960
    tail = bell * (poly * t - 0.3989422804 * size)
    return jnp.where(values >= 0.0, 1.0 - tail, tail)


def get_rows(ref, start, count, stride=None):
    return jnp.concatenate([ref[h, pl.ds(start, count, stride), :] for h in range(ref.shape[0])], axis=1)


def set_rows(ref, start, values, stride=None):
    for h in range(ref.shape[0]):
        ref[h, pl.ds(start, values.shape[0], stride), :] = values[:, h * LANES : (h + 1) * LANES]


def pitch(cols):
    return cols + 8 if cols % 16 == 0 else cols


def planes(rows, ch):
    return pltpu.VMEM((ch // LANES, rows, LANES), F32)


def conv_kernel(sizes, picked, edges, span, routes, gates, place_ref, x_far, left, right, top, bottom, grad_out_far, weight_far, tables,
                keep, give, grad_far, e_left, e_right,
                x, grad_out, weight, grad, shifted, patch, delta_a, delta_b, acc, ext, sums, lcol, rcol,
                weight_sems, field_sems):
    rows_dev, cols_dev, ch = x.shape
    experts = weight.shape[0]
    field_copies = [
        pltpu.make_async_copy(x_far, x, field_sems.at[0]),
        pltpu.make_async_copy(grad_out_far, grad_out, field_sems.at[1]),
    ]
    pieces = rows_dev // TILE

    def grad_copy(i):
        span = pl.ds(i * TILE, TILE)
        return pltpu.make_async_copy(grad.at[span], grad_far.at[span], field_sems.at[2 + i])


    def fetch(e):
        return pltpu.make_async_copy(weight_far.at[e], weight.at[e], weight_sems.at[e])

    def in_first(e):
        found = routes[0] == e - SHARED
        for k in range(1, picked):
            found = found | (routes[k] == e - SHARED)
        return found

    count = SHARED + picked
    early = list(range(SHARED)) + [routes[k] + SHARED for k in range(picked)]
    field_copies[0].start()
    for e in early[:2]:
        fetch(e).start()
    field_copies[1].start()

    slots, reals, groups, width, fold, virtual, per = sizes
    chips = keep.shape[0]
    across = cols_dev // TILE
    tiles = (rows_dev // TILE) * across
    area = TILE * TILE
    column = lax.broadcasted_iota(jnp.int32, (cols_dev, ch), 0)

    valid = neighbours(place_ref, edges)
    lcol[...] = left[...].astype(F32) * valid[0]
    rcol[...] = right[...].astype(F32) * valid[1]
    field_copies[0].wait()
    for e in early[2:4]:
        fetch(e).start()

    def put_row(at, row, low, high):
        shifted[1, at] = row.astype(BF16)
        shifted[0, at] = jnp.where(column == 0, low, pltpu.roll(row, 1, 0)).astype(BF16)
        shifted[2, at] = jnp.where(column == cols_dev - 1, high, pltpu.roll(row, cols_dev - 1, 0)).astype(BF16)

    def fill(step, carry):
        for sub in range(8):
            at = step * 8 + sub
            put_row(at + 1, x[at].astype(F32), lcol[pl.ds(at, 1), :], rcol[pl.ds(at, 1), :])
        return carry

    lax.fori_loop(0, rows_dev // 8, fill, 0)
    for ref, at, flag in ((top, 0, valid[2]), (bottom, rows_dev + 1, valid[3])):
        edge = ref[...].astype(F32) * flag
        low = edge[cols_dev : cols_dev + 1] * valid[0]
        high = edge[cols_dev + 1 : cols_dev + 2] * valid[1]
        put_row(at, edge[:cols_dev], low, high)

    def clear(at, carry):
        for b in range(3):
            acc[b, at] = jnp.zeros((cols_dev, ch), F32)
        return carry

    lax.fori_loop(0, rows_dev + 2, clear, 0)

    firsts = range(0, count, 2)

    def place(tile):
        return tile // across * TILE, pl.multiple_of(tile % across * TILE, TILE)

    def expert(tile, s):
        return s if s < SHARED else routes[tile * picked + s - SHARED] + SHARED

    def gather(tile):
        row, col = place(tile)
        for a in range(3):
            for b in range(3):
                tap = 3 * a + b
                patch[:, tap * ch : (tap + 1) * ch] = shifted[
                    b, pl.ds(row + a, TILE), pl.ds(col, TILE), :
                ].reshape(area, ch)

    def forward(tile, first):
        pair = range(first, min(first + 2, count))
        kernel = jnp.concatenate([weight[expert(tile, s)] for s in pair], axis=1)
        return jnp.dot(patch[...], kernel, preferred_element_type=F32)

    def slopes(tile, first, preact, delta):
        row, col = place(tile)
        upstream = grad_out[pl.ds(row, TILE), pl.ds(col, TILE), :].reshape(area, ch).astype(F32)
        for i, s in enumerate(range(first, min(first + 2, count))):
            slope = gelu_slope(preact[:, i * ch : (i + 1) * ch])
            delta[:, s * ch : (s + 1) * ch] = (gates[tile * count + s] * slope * upstream).astype(BF16)

    def backward(tile, a, delta):
        row, col = place(tile)
        total = None
        for s in range(count):
            part = lax.dot_general(
                delta[:, s * ch : (s + 1) * ch],
                weight[expert(tile, s), a * 3 * ch : (a + 1) * 3 * ch, :],
                NT,
                preferred_element_type=F32,
            )
            total = part if total is None else total + part
        for b in range(3):
            acc[b, pl.ds(row + a, TILE), pl.ds(col, TILE), :] += total[:, b * ch : (b + 1) * ch].reshape(
                TILE, TILE, ch
            )

    def step(tile, source, target):
        gather(tile + 1)
        for i, first in enumerate(firsts):
            preact = forward(tile + 1, first)
            for a in range(i, 3 if first == firsts[-1] else i + 1):
                backward(tile, a, source)
            slopes(tile + 1, first, preact, target)

    gather(0)
    for first in firsts:
        for e in early[first : first + 2]:
            fetch(e).wait()
        for e in early[first + 4 : first + 6]:
            fetch(e).start()
        if first == min(2, firsts[-1]):
            for e in range(SHARED, experts):

                @pl.when(jnp.logical_not(in_first(e)))
                def _():
                    fetch(e).start()

        preact = forward(0, first)
        if first == 0:
            field_copies[1].wait()
        slopes(0, first, preact, delta_a)
    for e in range(SHARED, experts):

        @pl.when(jnp.logical_not(in_first(e)))
        def _():
            fetch(e).wait()

    pairs = (tiles - 1) // 2

    def two(i, carry):
        step(2 * i, delta_a, delta_b)
        step(2 * i + 1, delta_b, delta_a)
        return carry

    lax.fori_loop(0, pairs, two, 0)
    last, source = 2 * pairs, delta_a
    if last < tiles - 1:
        step(last, delta_a, delta_b)
        last, source = last + 1, delta_b
    for a in range(3):
        backward(last, a, source)

    filler = jnp.zeros((virtual - cols_dev, ch), F32)

    def put_ext(at, inner):
        middle = acc[1, at] + inner if inner is not None else acc[1, at]
        total = jnp.concatenate([acc[0, at], filler], axis=0)
        total = total + pltpu.roll(jnp.concatenate([middle, filler], axis=0), 1, 0)
        total = total + pltpu.roll(jnp.concatenate([acc[2, at], filler], axis=0), 2, 0)
        set_rows(ext, pl.multiple_of(at * virtual, 8), total)
        return pltpu.roll(total, virtual - 1, 0)[:cols_dev]

    def join(step, carry):
        for sub in range(4):
            at = step * 4 + sub
            grad[at] = put_ext(at + 1, grad_out[at].astype(F32))
        return carry

    for i in range(pieces):
        lax.fori_loop(i * TILE // 4, (i + 1) * TILE // 4, join, 0)
        grad_copy(i).start()
    blocks = []
    for at in (0, rows_dev + 1):
        line = put_ext(at, None)
        corners = [get_rows(ext, at * virtual, 1), get_rows(ext, at * virtual + width - 1, 1)]
        line = jnp.concatenate([line, *corners, jnp.zeros((TILE - 2, ch), F32)], axis=0).astype(BF16)
        blocks += [line[i : i + TILE] for i in range(0, line.shape[0], TILE)]
    for i, block in enumerate(blocks):
        begin = (per + i // chips) * ch
        give[i % chips, :, begin : begin + ch] = block
    for ref, at in ((e_left, 0), (e_right, width - 1)):
        ref[...] = get_rows(ext, virtual + at, rows_dev, virtual).astype(BF16)

    row_table = tables[span]
    depth = row_table.shape[1]
    set_rows(ext, (rows_dev + 2) * virtual, jnp.zeros(((depth - rows_dev - 2) * virtual, ch), F32))
    sums[...] = jnp.zeros(sums.shape, F32)
    later = {}

    def emit(v, found):
        for half, ref in enumerate((keep, give)):
            for c in range(chips):
                begin = (half * chips + c) * reals
                parts = []
                for u in range(v, virtual, per):
                    if u < width:
                        parts.append(found[u][begin : begin + reals])
                    elif u < width + fold:
                        parts.append(get_rows(sums, u - width, reals, fold))
                    else:
                        parts.append(jnp.zeros((reals, ch), F32))
                ref[c, :, v * ch : (v + 1) * ch] = jnp.concatenate(parts, axis=0).astype(BF16)

    for v in range(per):
        wanted = [u for u in range(v, virtual, per) if u < width]
        cells = jnp.concatenate(
            [get_rows(ext, u, depth, virtual).astype(BF16) for u in wanted], axis=1
        )
        freqs = jnp.dot(row_table, cells, preferred_element_type=F32)
        found = {u: freqs[:, i * ch : (i + 1) * ch] for i, u in enumerate(wanted)}
        at = 2 * chips * reals
        for u in wanted:
            set_rows(sums, u, found[u][at : at + 1])
        if len(wanted) == groups:
            emit(v, found)
        else:
            later[v] = found
    for v, found in later.items():
        emit(v, found)
    for i in range(pieces):
        grad_copy(i).wait()


def neighbours(place, edges):
    gx, gy = place[0], place[1]
    found = (gy > 0, gy < edges[1] - 1, gx > 0, gx < edges[0] - 1)
    return [jnp.where(flag, 1.0, 0.0) for flag in found]


def edge_blocks(cols_dev):
    return cols_dev // TILE + 1


def find_edge(gift, chips, per, ch, blocks, which):
    parts = []
    for i in range(which * blocks, (which + 1) * blocks):
        begin = (per + i // chips) * ch
        parts.append(gift[i % chips, :, begin : begin + ch])
    return jnp.concatenate(parts, axis=1)


def regroup_kernel(sizes, chips, here, edges, span, place, gift, e_left, e_right, tables, *refs):
    slots, reals, groups, width, fold, virtual, per = sizes
    parts, (above, below, *outs, rows) = refs[:chips], refs[chips:]
    cols_dev, ch = above.shape
    rows_dev = e_left.shape[0]
    blocks = edge_blocks(cols_dev)
    set_rows(rows, reals * virtual, jnp.zeros((virtual, ch), F32))
    for v in range(per):
        total = None
        for part in parts:
            piece = part[:, v * ch : (v + 1) * ch].astype(F32)
            total = piece if total is None else total + piece
        for i, u in enumerate(range(v, virtual, per)):
            piece = total[i * reals : (i + 1) * reals]
            set_rows(rows, u, piece, virtual)
            if width <= u < width + fold:
                set_rows(rows, reals * virtual + u - width, piece, fold)
    plain = get_rows(rows, reals * virtual, virtual).astype(BF16)
    low = jnp.dot(tables[span], plain, preferred_element_type=F32)
    share = low.shape[0] // 4
    for real in range(reals):
        part = real % 2 * share
        set_rows(rows, real * virtual + width, low[part : part + share])

    valid = neighbours(place, edges)
    first_core = place[0] % 2 == 0

    def line(far, near, flag):
        flat = jnp.where(first_core, far.astype(F32), near.astype(F32)) * flag
        return [flat[:, i * ch : (i + 1) * ch] for i in range(blocks)]

    far_bottom = parts[1][:, per * ch : (per + blocks) * ch]
    far_top = parts[chips - 1][:, per * ch : (per + blocks) * ch]
    from_above = line(far_bottom, find_edge(gift, chips, per, ch, blocks, 1), valid[2])
    from_below = line(find_edge(gift, chips, per, ch, blocks, 0), far_top, valid[3])
    above[...] = jnp.concatenate(from_above[:-1], axis=0).astype(BF16)
    below[...] = jnp.concatenate(from_below[:-1], axis=0).astype(BF16)
    row = lax.broadcasted_iota(jnp.int32, (rows_dev, ch), 0)
    sides = []
    for ref, at in ((e_right, 1), (e_left, 0)):
        side = ref[...].astype(F32)
        side = side + jnp.where(row == 0, from_above[-1][at : at + 1], 0.0)
        sides.append(side + jnp.where(row == rows_dev - 1, from_below[-1][at : at + 1], 0.0))

    for place in range(slots // here):
        block = [get_rows(rows, 2 * place * here * virtual, 2 * here * virtual)]
        if outs[place].shape[0] > block[0].shape[0]:
            block.append(sides[0] if place == 1 else sides[1])
        outs[place][...] = jnp.concatenate(block, axis=0).astype(BF16)
    if here == slots:
        for ref, side in zip(outs[1:], sides):
            ref[...] = side.astype(BF16)


def modes_kernel(sizes, split, scale, back_scale, sources, place, col_table, back_table, ids, bands, *refs):
    slots, reals, groups, width, fold, virtual, per = sizes
    parts, (low_out, *outs) = refs[:sources], refs[sources:]
    ch = low_out.shape[1]
    share = low_out.shape[0] // 4
    here = parts[0].shape[0] // (2 * virtual)
    cols_dev = outs[0].shape[0] // (2 * here)
    first = place[0] * slots + (place[1] * here if split else 0)

    def bands_of(row, rows, begin):
        line = jnp.broadcast_to(ids[pl.ds(row, 1), :], (rows, KW))
        wanted = lax.broadcasted_iota(jnp.int32, (rows, KW), 0) % KW + begin
        at = lax.broadcasted_iota(jnp.int32, (rows, KW), 1)
        return jnp.sum(jnp.where(wanted == at, line, 0).astype(F32), axis=1, keepdims=True)

    low_line = bands_of(0, share, place[0] * share)
    for s in range(here):
        blocks = [part[2 * s * virtual : 2 * (s + 1) * virtual].astype(F32) for part in parts]
        cosine = jnp.concatenate([block[:virtual] for block in blocks], axis=0)
        sine = jnp.concatenate([block[virtual:] for block in blocks], axis=0)
        cells = jnp.concatenate([cosine, sine], axis=1).astype(BF16)
        freqs = jnp.dot(col_table[...], cells, preferred_element_type=F32)
        over_cos, over_sin = freqs[:KW], freqs[KW:]
        slot = first + s
        plus = jnp.where(slot == 0, 0.0, scale)
        low = sum(blocks)
        coefs = jnp.concatenate(
            [
                (over_cos[:, :ch] - over_sin[:, ch:]) * plus,
                (over_cos[:, :ch] + over_sin[:, ch:]) * scale,
                (over_cos[:, ch:] + over_sin[:, :ch]) * plus,
                (over_sin[:, :ch] - over_cos[:, ch:]) * scale,
                low[width : width + share] * scale,
                low[virtual + width : virtual + width + share] * scale,
                jnp.zeros((2 * share, ch), F32),
            ],
            axis=0,
        ).astype(BF16)
        plus_line = bands_of(slot, KW, 0)
        minus_line = bands_of(jnp.where(slot == 0, KH // 2, KH - slot), KW, 0)
        band = jnp.concatenate([plus_line, minus_line, plus_line, minus_line] + [low_line] * 4, axis=0)
        mixed = None
        for b in range(bands.shape[0]):
            chosen = jnp.where(band == float(b), coefs, jnp.zeros_like(coefs))
            part = lax.dot_general(chosen, bands[b], NT, preferred_element_type=F32)
            mixed = part if mixed is None else mixed + part
        mixed = (mixed * back_scale).astype(BF16)
        if s == 0:
            low_out[...] = mixed[4 * KW :]
        plus_cos, minus_cos = mixed[:KW], mixed[KW : 2 * KW]
        plus_sin, minus_sin = mixed[2 * KW : 3 * KW], mixed[3 * KW : 4 * KW]
        sides = jnp.concatenate(
            [
                jnp.concatenate([plus_cos, plus_sin, minus_cos, minus_sin], axis=0),
                jnp.concatenate([plus_sin, -plus_cos, -minus_sin, minus_cos], axis=0),
            ],
            axis=1,
        )
        field = jnp.dot(back_table[...], sides, preferred_element_type=F32).astype(BF16)
        for z, out in enumerate(outs):
            span = slice(z * cols_dev, (z + 1) * cols_dev)
            begin = 2 * s * cols_dev
            out[begin : begin + cols_dev] = field[span, :ch]
            out[begin + cols_dev : begin + 2 * cols_dev] = field[span, ch:]


def final_kernel(count, main, edges, spans, place, tables, grad_far, left, right, above, below, *refs):
    blocks, (out, grad, rows, cells, lcol, rcol, sem) = refs[:count], refs[count:]
    rows_dev, cols_dev, ch = out.shape
    apart = pitch(cols_dev)
    table, low_table = tables[spans[0]], tables[spans[1]]
    depth = table.shape[1]
    valid = neighbours(place, edges)
    grad_copy = pltpu.make_async_copy(grad_far, grad, sem)
    grad_copy.start()
    for place, block in enumerate(blocks):
        for i in range(main // cols_dev):
            line = block[i * cols_dev : (i + 1) * cols_dev].astype(F32)
            set_rows(rows, (place * (main // cols_dev) + i) * apart, line)
    used = count * (main // cols_dev)
    low = jnp.concatenate([block[main:] for block in blocks], axis=0)
    set_rows(rows, used * apart, jnp.dot(low_table, low, preferred_element_type=F32))
    set_rows(rows, (used + 1) * apart, jnp.zeros((rows.shape[1] - (used + 1) * apart, ch), F32))
    lcol[...] = left[left.shape[0] - rows_dev :].astype(F32) * valid[0]
    rcol[...] = right[right.shape[0] - rows_dev :].astype(F32) * valid[1]
    for w in range(0, cols_dev, 2):
        modes = jnp.concatenate(
            [get_rows(rows, w + i, depth, apart).astype(BF16) for i in range(2)], axis=1
        )
        lines = jnp.dot(table, modes, preferred_element_type=F32)
        for i in range(2):
            set_rows(cells, w + i, lines[:, i * ch : (i + 1) * ch], apart)
    column = lax.broadcasted_iota(jnp.int32, (cols_dev, ch), 0)

    def total(at):
        line = get_rows(cells, pl.multiple_of(at * apart, 8), cols_dev) + grad[at]
        line = line + jnp.where(column == 0, lcol[pl.ds(at, 1), :], 0.0)
        return line + jnp.where(column == cols_dev - 1, rcol[pl.ds(at, 1), :], 0.0)

    grad_copy.wait()

    def store(step, carry):
        for sub in range(4):
            at = step * 4 + sub
            out[at] = total(at).astype(BF16)
        return carry

    lax.fori_loop(0, rows_dev // 4, store, 0)
    out[0] = (total(0) + above[...].astype(F32)).astype(BF16)
    last = rows_dev - 1
    out[last] = (total(last) + below[...].astype(F32)).astype(BF16)


def in_vmem():
    return pl.BlockSpec(memory_space=pltpu.VMEM)


def in_hbm():
    return pl.BlockSpec(memory_space=pltpu.HBM)


def in_smem():
    return pl.BlockSpec(memory_space=pltpu.SMEM)


def call(kernel, out_shapes, in_specs, scratch, name, limit, out_specs=None):
    many = isinstance(out_shapes, (list, tuple))
    return pl.pallas_call(
        kernel,
        out_shape=out_shapes,
        in_specs=in_specs,
        out_specs=out_specs or ([in_vmem() for _ in out_shapes] if many else in_vmem()),
        scratch_shapes=scratch,
        compiler_params=pltpu.CompilerParams(vmem_limit_bytes=limit << 20),
        name=name,
    )


def cos_sin(product, period):
    theta = (product % period) * (2.0 * math.pi / period)
    return np.cos(theta), np.sin(theta)


def padded(table, rows, cols):
    return np.pad(table, ((0, rows - table.shape[0]), (0, cols - table.shape[1])))


def angle_tables(n_gx, n_gy, rows_dev, cols_dev):
    sizes = layout(n_gx, cols_dev)
    slots, reals, groups, width, fold, virtual, per = sizes
    chips, share = n_gx // 2, KW // n_gx
    split = slots % n_gy == 0
    here = slots // n_gy if split else slots
    full_rows, full_cols = rows_dev * n_gx, cols_dev * n_gy
    used = 2 * chips * reals
    depth_in, depth_out = round_up(rows_dev + 2, 16), round_up(used + 1, 16)
    modes = np.arange(KW)
    chip_ids = np.arange(chips)

    def row_angles(rows, freqs):
        cosine, sine = cos_sin(rows[:, None] * freqs[None, :], full_rows)
        table = np.stack([cosine, sine], axis=2).reshape(len(rows), used)
        ones = np.ones((len(rows), 1))
        return np.concatenate([table, ones, np.zeros((len(rows), depth_out - used - 1))], axis=1)

    def low_angles(cols, owners):
        product = (owners[:, None] * share + np.arange(share)[None, :])[None] * cols[:, None, None]
        cosine, sine = cos_sin(product, full_cols)
        spare = np.zeros_like(cosine)
        return np.concatenate([cosine, sine, spare, spare], axis=2)

    def owners_of(order, core):
        return np.concatenate([2 * order + core, 2 * order + 1 - core])

    both, forth, back = [], [], []
    wide = np.arange(virtual)
    for gy in range(n_gy):
        sources = (gy - np.arange(n_gy)) % n_gy if split else np.arange(n_gy)
        ext_cols = sources[:, None] * cols_dev - 1 + wide[None, :]
        inside = (ext_cols >= 0) & (ext_cols < full_cols) & (wide < width)[None, :]
        cosine, sine = cos_sin(modes[:, None] * ext_cols.reshape(1, -1), full_cols)
        forth.append(np.concatenate([cosine, sine]) * inside.reshape(1, -1))
        all_cols = (sources[:, None] * cols_dev + np.arange(cols_dev)[None, :]).reshape(-1, 1)
        back.append(np.concatenate(cos_sin(all_cols * modes[None, :], full_cols) * 2, axis=1))
    for gx in range(n_gx):
        chip, core = gx // 2, gx % 2
        for gy in range(n_gy):
            places = np.arange(slots)
            if split:
                places = (places + gy * here) % slots

            def frequencies(owners):
                ids = (owners[:, None] * slots + places[None, :]).reshape(-1)
                return np.where(ids == 0, KH // 2, ids)

            order = (chip_ids + chip) % chips
            ext_rows = gx * rows_dev - 1 + np.arange(depth_in)
            inside = (ext_rows >= 0) & (ext_rows < full_rows) & (np.arange(depth_in) < rows_dev + 2)
            row_table = (row_angles(ext_rows, frequencies(owners_of(order, core))) * inside[:, None]).T
            owners = owners_of((chip - chip_ids) % chips, core)
            back_rows = row_angles(gx * rows_dev + np.arange(rows_dev), frequencies(owners))
            cols = gy * cols_dev - 1 + wide
            inside = (cols >= 0) & (cols < full_cols) & (wide < width)
            low_table = (low_angles(cols, np.array([gx]))[:, 0] * inside[:, None]).T
            back_low = low_angles(gy * cols_dev + np.arange(cols_dev), owners).reshape(cols_dev, -1)
            tables = [row_table, back_rows, low_table, back_low]
            lanes = round_up(max(table.shape[1] for table in tables), LANES)
            both.append(np.concatenate([padded(t, round_up(len(t), 16), lanes) for t in tables]))
    both = np.stack(both).reshape(n_gx, n_gy, *both[0].shape)
    return [np.asarray(table, np.float32).astype(BF16) for table in (both, np.stack(forth), np.stack(back))]


def table_spans(sizes, rows_dev, cols_dev, n_gx):
    slots, reals, groups, width, fold, virtual, per = sizes
    used, share = n_gx * reals, KW // n_gx
    shapes = [
        (round_up(used + 1, 16), round_up(rows_dev + 2, 16)),
        (rows_dev, round_up(used + 1, 16)),
        (4 * share, virtual),
        (cols_dev, n_gx * 4 * share),
    ]
    spans, begin = [], 0
    for rows, cols in shapes:
        spans.append((slice(begin, begin + rows), slice(0, cols)))
        begin += round_up(rows, 16)
    return spans


def body(saved_mid, out_grad, expert_weight, routes, gates, band_matrix, band_ids):
    rows_dev, cols_dev, ch = saved_mid.shape
    n_gx, n_gy = lax.axis_size("gx"), lax.axis_size("gy")
    gx, gy = lax.axis_index("gx"), lax.axis_index("gy")
    full_rows, full_cols = rows_dev * n_gx, cols_dev * n_gy
    sizes = layout(n_gx, cols_dev)
    slots, reals, groups, width, fold, virtual, per = sizes
    chips = n_gx // 2
    swap = [(i, i ^ 1) for i in range(n_gx)]
    experts = expert_weight.shape[0]

    def ring(array, axis, step):
        count = lax.axis_size(axis)
        return lax.ppermute(array, axis, [(i, (i + step) % count) for i in range(count)])

    def shape(*dims, dtype=BF16):
        return jax.ShapeDtypeStruct(dims, dtype)

    split = slots % n_gy == 0
    here = slots // n_gy if split else slots
    depth_in, depth_out = round_up(rows_dev + 2, 16), round_up(n_gx * reals + 1, 16)
    spans = table_spans(sizes, rows_dev, cols_dev, n_gx)
    tables, col_tables, back_tables = angle_tables(n_gx, n_gy, rows_dev, cols_dev)
    tables = jnp.asarray(tables)[gx, gy]
    col_table, back_table = jnp.asarray(col_tables)[gy], jnp.asarray(back_tables)[gy]
    share = KW // n_gx
    place = jnp.stack([gx, gy]).astype(jnp.int32)
    edges = (n_gx, n_gy)

    left = ring(saved_mid[:, cols_dev - 1, :], "gy", 1)
    right = ring(saved_mid[:, 0, :], "gy", -1)

    def edge_row(at):
        return jnp.concatenate([saved_mid[at], left[at : at + 1], right[at : at + 1]], axis=0)

    bottom = ring(edge_row(0), "gx", -1)
    top = ring(edge_row(rows_dev - 1), "gx", 1)

    picked = routes.shape[2]
    packed = per * ch
    lines = edge_blocks(cols_dev)
    extra = -(-2 * lines // chips) * ch
    keep, give, grad, e_left, e_right = call(
        functools.partial(conv_kernel, sizes, picked, edges, spans[0]),
        [
            shape(chips, groups * reals, packed),
            shape(chips, groups * reals, packed + extra),
            pltpu.HBM((rows_dev, cols_dev, ch), F32),
            shape(rows_dev, ch),
            shape(rows_dev, ch),
        ],
        [in_smem()] * 3 + [in_hbm()] + [in_vmem()] * 4 + [in_hbm()] * 2 + [in_vmem()],
        [
            pltpu.VMEM((rows_dev, cols_dev, ch), BF16),
            pltpu.VMEM((rows_dev, cols_dev, ch), BF16),
            pltpu.VMEM((experts, 9 * ch, ch), BF16),
            pltpu.VMEM((rows_dev, cols_dev, ch), F32),
            pltpu.VMEM((3, rows_dev + 2, cols_dev, ch), BF16),
            pltpu.VMEM((TILE * TILE, 9 * ch), BF16),
            pltpu.VMEM((TILE * TILE, (SHARED + picked) * ch), BF16),
            pltpu.VMEM((TILE * TILE, (SHARED + picked) * ch), BF16),
            pltpu.VMEM((3, rows_dev + 2, cols_dev, ch), F32),
            planes(depth_in * virtual, ch),
            planes(round_up(max(width, reals * fold), 8), ch),
            pltpu.VMEM((rows_dev, ch), F32),
            pltpu.VMEM((rows_dev, ch), F32),
            pltpu.SemaphoreType.DMA((experts,)),
            pltpu.SemaphoreType.DMA((2 + rows_dev // TILE,)),
        ],
        "conv",
        40,
        [in_vmem()] * 2 + [in_hbm()] + [in_vmem()] * 2,
    )(
        routes.reshape(-1),
        gates.reshape(-1),
        place,
        pltpu.with_memory_space_constraint(saved_mid, pltpu.HBM),
        left,
        right,
        top,
        bottom,
        pltpu.with_memory_space_constraint(out_grad, pltpu.HBM),
        pltpu.with_memory_space_constraint(expert_weight.reshape(experts, 9 * ch, ch), pltpu.HBM),
        tables,
    )

    gift = lax.ppermute(give, "gx", swap)
    messages = [(keep[d].astype(F32) + gift[d, :, :packed].astype(F32)).astype(BF16) for d in range(chips)]
    for d, which in ((1, 1), (chips - 1, 0)):
        edge = find_edge(gift, chips, per, ch, lines, which)
        messages[d] = jnp.concatenate([messages[d], edge], axis=1)
    parts = [messages[0]] + [ring(messages[d], "gx", 2 * d) for d in range(1, chips)]
    block_rows = here * 2 * virtual
    if split:
        ends = [rows_dev if d in (1, n_gy - 1) else 0 for d in range(n_gy)]
        regrouped = [shape(block_rows + end, ch) for end in ends]
    else:
        regrouped = [shape(block_rows, ch), shape(rows_dev, ch), shape(rows_dev, ch)]
    from_above, from_below, *regrouped = call(
        functools.partial(regroup_kernel, sizes, chips, here, edges, spans[2]),
        [shape(cols_dev, ch), shape(cols_dev, ch), *regrouped],
        [in_smem()] + [in_vmem()] * (4 + chips),
        [planes((reals + 1) * virtual, ch)],
        "regroup",
        8,
    )(place, gift, e_left, e_right, tables, *parts)

    if split:
        cells = [regrouped[0]] + [ring(regrouped[d], "gy", d) for d in range(1, n_gy)]
        from_left, from_right = cells[1], cells[n_gy - 1]
    else:
        gathered = lax.all_gather(regrouped[0], "gy", axis=0)
        cells = [gathered[z] for z in range(n_gy)]
        from_left, from_right = ring(regrouped[1], "gy", 1), ring(regrouped[2], "gy", -1)
    low_modes, *mixed = call(
        functools.partial(
            modes_kernel,
            sizes,
            split,
            1.0 / math.sqrt(full_rows * full_cols),
            1.0 / math.sqrt(2 * KH * KW),
            n_gy,
        ),
        [shape(4 * share, ch)] + [shape(here * 2 * cols_dev, ch) for _ in range(n_gy)],
        [in_smem()] + [in_vmem()] * (4 + n_gy),
        [],
        "modes",
        12,
    )(place, col_table, back_table, band_ids, band_matrix, *cells)
    if split:
        mixed = [mixed[0]] + [ring(mixed[d], "gy", -d) for d in range(1, n_gy)]
    else:
        mixed = [lax.dynamic_index_in_dim(jnp.stack(mixed), gy, 0, keepdims=False)]
    block = jnp.concatenate([*mixed, low_modes], axis=0)

    blocks = [block] + [ring(block, "gx", 2 * d) for d in range(1, chips)]
    blocks = blocks + [lax.ppermute(array, "gx", swap) for array in blocks]
    return call(
        functools.partial(final_kernel, n_gx, slots * 2 * cols_dev, edges, (spans[1], spans[3])),
        shape(rows_dev, cols_dev, ch),
        [in_smem(), in_vmem(), in_hbm()] + [in_vmem()] * (4 + n_gx),
        [
            pltpu.VMEM((rows_dev, cols_dev, ch), F32),
            planes(depth_out * pitch(cols_dev), ch),
            planes(rows_dev * pitch(cols_dev), ch),
            pltpu.VMEM((rows_dev, ch), F32),
            pltpu.VMEM((rows_dev, ch), F32),
            pltpu.SemaphoreType.DMA,
        ],
        "final",
        16,
    )(place, tables, grad, from_left, from_right, from_above, from_below, *blocks)


def solution(mesh):
    placed = (
        P("gx", "gy", None),
        P("gx", "gy", None),
        P(),
        P("gx", "gy", None),
        P("gx", "gy", None),
        P(),
        P(),
    )
    return jax.shard_map(
        body, mesh=mesh, in_specs=placed, out_specs=P("gx", "gy", None), check_vma=False
    )
```

```python
import functools
import math

import jax
import jax.numpy as jnp
import numpy as np
from jax import lax
from jax.experimental import pallas as pl
from jax.experimental.pallas import tpu as pltpu
from jax.sharding import PartitionSpec as P

SHARED = 2
TILE = 16
KH = 64
KW = 32
LANES = 128
F32 = jnp.float32
BF16 = jnp.bfloat16
NT = (((1,), (1,)), ((), ()))


def round_up(value, unit):
    return -(-value // unit) * unit


def layout(mesh_rows, cols_dev):
    slots = KH // 2 // mesh_rows
    reals = 2 * slots
    groups = max(1, 16 // reals)
    width = cols_dev + 2
    fold = -(-width // reals)
    unit = 8 * groups // math.gcd(8, groups)
    virtual = round_up(max(width + fold, reals * fold), unit)
    return slots, reals, groups, width, fold, virtual, virtual // groups


def gelu_slope(values):
    size = jnp.abs(values)
    t = 1.0 / (1.0 + 0.23164189 * size)
    bell = jnp.exp2(values * (values * -0.7213475204444817))
    poly = 0.5307027145 * t - 0.7265760135
    poly = poly * t + 0.7107068705
    poly = poly * t - 0.1422483680
    poly = poly * t + 0.1274147960
    tail = bell * (poly * t - 0.3989422804 * size)
    return jnp.where(values >= 0.0, 1.0 - tail, tail)


def get_rows(ref, start, count, stride=None):
    return jnp.concatenate([ref[h, pl.ds(start, count, stride), :] for h in range(ref.shape[0])], axis=1)


def set_rows(ref, start, values, stride=None):
    for h in range(ref.shape[0]):
        ref[h, pl.ds(start, values.shape[0], stride), :] = values[:, h * LANES : (h + 1) * LANES]


def pitch(cols):
    return cols + 8 if cols % 16 == 0 else cols


def planes(rows, ch):
    return pltpu.VMEM((ch // LANES, rows, LANES), F32)


def conv_kernel(sizes, picked, edges, span, routes, gates, place_ref, x_far, left, right, top, bottom, grad_out_far, weight_far, tables,
                keep, give, grad_far, e_left, e_right,
                x, grad_out, weight, grad, shifted, patch, delta_a, delta_b, acc, ext, sums, lcol, rcol,
                weight_sems, field_sems):
    rows_dev, cols_dev, ch = x.shape
    experts = weight.shape[0]
    field_copies = [
        pltpu.make_async_copy(x_far, x, field_sems.at[0]),
        pltpu.make_async_copy(grad_out_far, grad_out, field_sems.at[1]),
    ]
    pieces = rows_dev // TILE

    def grad_copy(i):
        span = pl.ds(i * TILE, TILE)
        return pltpu.make_async_copy(grad.at[span], grad_far.at[span], field_sems.at[2 + i])


    def fetch(e):
        return pltpu.make_async_copy(weight_far.at[e], weight.at[e], weight_sems.at[e])

    def in_first(e):
        found = routes[0] == e - SHARED
        for k in range(1, picked):
            found = found | (routes[k] == e - SHARED)
        return found

    count = SHARED + picked
    early = list(range(SHARED)) + [routes[k] + SHARED for k in range(picked)]
    field_copies[0].start()
    for e in early[:2]:
        fetch(e).start()
    field_copies[1].start()

    slots, reals, groups, width, fold, virtual, per = sizes
    chips = keep.shape[0]
    across = cols_dev // TILE
    tiles = (rows_dev // TILE) * across
    area = TILE * TILE
    column = lax.broadcasted_iota(jnp.int32, (cols_dev, ch), 0)

    valid = neighbours(place_ref, edges)
    lcol[...] = left[...].astype(F32) * valid[0]
    rcol[...] = right[...].astype(F32) * valid[1]
    field_copies[0].wait()
    for e in early[2:4]:
        fetch(e).start()

    def put_row(at, row, low, high):
        shifted[1, at] = row.astype(BF16)
        shifted[0, at] = jnp.where(column == 0, low, pltpu.roll(row, 1, 0)).astype(BF16)
        shifted[2, at] = jnp.where(column == cols_dev - 1, high, pltpu.roll(row, cols_dev - 1, 0)).astype(BF16)

    def fill(step, carry):
        for sub in range(8):
            at = step * 8 + sub
            put_row(at + 1, x[at].astype(F32), lcol[pl.ds(at, 1), :], rcol[pl.ds(at, 1), :])
        return carry

    lax.fori_loop(0, rows_dev // 8, fill, 0)
    for ref, at, flag in ((top, 0, valid[2]), (bottom, rows_dev + 1, valid[3])):
        edge = ref[...].astype(F32) * flag
        low = edge[cols_dev : cols_dev + 1] * valid[0]
        high = edge[cols_dev + 1 : cols_dev + 2] * valid[1]
        put_row(at, edge[:cols_dev], low, high)

    def clear(at, carry):
        for b in range(3):
            acc[b, at] = jnp.zeros((cols_dev, ch), F32)
        return carry

    lax.fori_loop(0, rows_dev + 2, clear, 0)

    firsts = range(0, count, 2)

    def place(tile):
        return tile // across * TILE, pl.multiple_of(tile % across * TILE, TILE)

    def expert(tile, s):
        return s if s < SHARED else routes[tile * picked + s - SHARED] + SHARED

    def gather(tile):
        row, col = place(tile)
        for a in range(3):
            for b in range(3):
                tap = 3 * a + b
                patch[:, tap * ch : (tap + 1) * ch] = shifted[
                    b, pl.ds(row + a, TILE), pl.ds(col, TILE), :
                ].reshape(area, ch)

    def forward(tile, first):
        pair = range(first, min(first + 2, count))
        kernel = jnp.concatenate([weight[expert(tile, s)] for s in pair], axis=1)
        return jnp.dot(patch[...], kernel, preferred_element_type=F32)

    def slopes(tile, first, preact, delta):
        row, col = place(tile)
        upstream = grad_out[pl.ds(row, TILE), pl.ds(col, TILE), :].reshape(area, ch).astype(F32)
        for i, s in enumerate(range(first, min(first + 2, count))):
            slope = gelu_slope(preact[:, i * ch : (i + 1) * ch])
            delta[:, s * ch : (s + 1) * ch] = (gates[tile * count + s] * slope * upstream).astype(BF16)

    def backward(tile, a, delta):
        row, col = place(tile)
        total = None
        for s in range(count):
            part = lax.dot_general(
                delta[:, s * ch : (s + 1) * ch],
                weight[expert(tile, s), a * 3 * ch : (a + 1) * 3 * ch, :],
                NT,
                preferred_element_type=F32,
            )
            total = part if total is None else total + part
        for b in range(3):
            acc[b, pl.ds(row + a, TILE), pl.ds(col, TILE), :] += total[:, b * ch : (b + 1) * ch].reshape(
                TILE, TILE, ch
            )

    def step(tile, source, target):
        gather(tile + 1)
        for i, first in enumerate(firsts):
            preact = forward(tile + 1, first)
            slopes(tile + 1, first, preact, target)
            for a in range(i, 3 if first == firsts[-1] else i + 1):
                backward(tile, a, source)

    gather(0)
    for first in firsts:
        for e in early[first : first + 2]:
            fetch(e).wait()
        for e in early[first + 4 : first + 6]:
            fetch(e).start()
        if first == min(2, firsts[-1]):
            for e in range(SHARED, experts):

                @pl.when(jnp.logical_not(in_first(e)))
                def _():
                    fetch(e).start()

        preact = forward(0, first)
        if first == 0:
            field_copies[1].wait()
        slopes(0, first, preact, delta_a)
    for e in range(SHARED, experts):

        @pl.when(jnp.logical_not(in_first(e)))
        def _():
            fetch(e).wait()

    pairs = (tiles - 1) // 2

    def two(i, carry):
        step(2 * i, delta_a, delta_b)
        step(2 * i + 1, delta_b, delta_a)
        return carry

    lax.fori_loop(0, pairs, two, 0)
    last, source = 2 * pairs, delta_a
    if last < tiles - 1:
        step(last, delta_a, delta_b)
        last, source = last + 1, delta_b
    for a in range(3):
        backward(last, a, source)

    filler = jnp.zeros((virtual - cols_dev, ch), F32)

    def put_ext(at, inner):
        middle = acc[1, at] + inner if inner is not None else acc[1, at]
        total = jnp.concatenate([acc[0, at], filler], axis=0)
        total = total + pltpu.roll(jnp.concatenate([middle, filler], axis=0), 1, 0)
        total = total + pltpu.roll(jnp.concatenate([acc[2, at], filler], axis=0), 2, 0)
        set_rows(ext, pl.multiple_of(at * virtual, 8), total)
        return pltpu.roll(total, virtual - 1, 0)[:cols_dev]

    def join(step, carry):
        for sub in range(4):
            at = step * 4 + sub
            grad[at] = put_ext(at + 1, grad_out[at].astype(F32))
        return carry

    for i in range(pieces):
        lax.fori_loop(i * TILE // 4, (i + 1) * TILE // 4, join, 0)
        grad_copy(i).start()
    blocks = []
    for at in (0, rows_dev + 1):
        line = put_ext(at, None)
        corners = [get_rows(ext, at * virtual, 1), get_rows(ext, at * virtual + width - 1, 1)]
        line = jnp.concatenate([line, *corners, jnp.zeros((TILE - 2, ch), F32)], axis=0).astype(BF16)
        blocks += [line[i : i + TILE] for i in range(0, line.shape[0], TILE)]
    for i, block in enumerate(blocks):
        begin = (per + i // chips) * ch
        give[i % chips, :, begin : begin + ch] = block
    for ref, at in ((e_left, 0), (e_right, width - 1)):
        ref[...] = get_rows(ext, virtual + at, rows_dev, virtual).astype(BF16)

    row_table = tables[span]
    depth = row_table.shape[1]
    set_rows(ext, (rows_dev + 2) * virtual, jnp.zeros(((depth - rows_dev - 2) * virtual, ch), F32))
    sums[...] = jnp.zeros(sums.shape, F32)
    later = {}

    def emit(v, found):
        for half, ref in enumerate((keep, give)):
            for c in range(chips):
                begin = (half * chips + c) * reals
                parts = []
                for u in range(v, virtual, per):
                    if u < width:
                        parts.append(found[u][begin : begin + reals])
                    elif u < width + fold:
                        parts.append(get_rows(sums, u - width, reals, fold))
                    else:
                        parts.append(jnp.zeros((reals, ch), F32))
                ref[c, :, v * ch : (v + 1) * ch] = jnp.concatenate(parts, axis=0).astype(BF16)

    for v in range(per):
        wanted = [u for u in range(v, virtual, per) if u < width]
        cells = jnp.concatenate(
            [get_rows(ext, u, depth, virtual).astype(BF16) for u in wanted], axis=1
        )
        freqs = jnp.dot(row_table, cells, preferred_element_type=F32)
        found = {u: freqs[:, i * ch : (i + 1) * ch] for i, u in enumerate(wanted)}
        at = 2 * chips * reals
        for u in wanted:
            set_rows(sums, u, found[u][at : at + 1])
        if len(wanted) == groups:
            emit(v, found)
        else:
            later[v] = found
    for v, found in later.items():
        emit(v, found)
    for i in range(pieces):
        grad_copy(i).wait()


def neighbours(place, edges):
    gx, gy = place[0], place[1]
    found = (gy > 0, gy < edges[1] - 1, gx > 0, gx < edges[0] - 1)
    return [jnp.where(flag, 1.0, 0.0) for flag in found]


def edge_blocks(cols_dev):
    return cols_dev // TILE + 1


def find_edge(gift, chips, per, ch, blocks, which):
    parts = []
    for i in range(which * blocks, (which + 1) * blocks):
        begin = (per + i // chips) * ch
        parts.append(gift[i % chips, :, begin : begin + ch])
    return jnp.concatenate(parts, axis=1)


def regroup_kernel(sizes, chips, here, edges, span, place, gift, e_left, e_right, tables, *refs):
    slots, reals, groups, width, fold, virtual, per = sizes
    parts, (above, below, *outs, rows) = refs[:chips], refs[chips:]
    cols_dev, ch = above.shape
    rows_dev = e_left.shape[0]
    blocks = edge_blocks(cols_dev)
    set_rows(rows, reals * virtual, jnp.zeros((virtual, ch), F32))
    for v in range(per):
        total = None
        for part in parts:
            piece = part[:, v * ch : (v + 1) * ch].astype(F32)
            total = piece if total is None else total + piece
        for i, u in enumerate(range(v, virtual, per)):
            piece = total[i * reals : (i + 1) * reals]
            set_rows(rows, u, piece, virtual)
            if width <= u < width + fold:
                set_rows(rows, reals * virtual + u - width, piece, fold)
    plain = get_rows(rows, reals * virtual, virtual).astype(BF16)
    low = jnp.dot(tables[span], plain, preferred_element_type=F32)
    share = low.shape[0] // 4
    for real in range(reals):
        part = real % 2 * share
        set_rows(rows, real * virtual + width, low[part : part + share])

    valid = neighbours(place, edges)
    first_core = place[0] % 2 == 0

    def line(far, near, flag):
        flat = jnp.where(first_core, far.astype(F32), near.astype(F32)) * flag
        return [flat[:, i * ch : (i + 1) * ch] for i in range(blocks)]

    far_bottom = parts[1][:, per * ch : (per + blocks) * ch]
    far_top = parts[chips - 1][:, per * ch : (per + blocks) * ch]
    from_above = line(far_bottom, find_edge(gift, chips, per, ch, blocks, 1), valid[2])
    from_below = line(find_edge(gift, chips, per, ch, blocks, 0), far_top, valid[3])
    above[...] = jnp.concatenate(from_above[:-1], axis=0).astype(BF16)
    below[...] = jnp.concatenate(from_below[:-1], axis=0).astype(BF16)
    row = lax.broadcasted_iota(jnp.int32, (rows_dev, ch), 0)
    sides = []
    for ref, at in ((e_right, 1), (e_left, 0)):
        side = ref[...].astype(F32)
        side = side + jnp.where(row == 0, from_above[-1][at : at + 1], 0.0)
        sides.append(side + jnp.where(row == rows_dev - 1, from_below[-1][at : at + 1], 0.0))

    for place in range(slots // here):
        block = [get_rows(rows, 2 * place * here * virtual, 2 * here * virtual)]
        if outs[place].shape[0] > block[0].shape[0]:
            block.append(sides[0] if place == 1 else sides[1])
        outs[place][...] = jnp.concatenate(block, axis=0).astype(BF16)
    if here == slots:
        for ref, side in zip(outs[1:], sides):
            ref[...] = side.astype(BF16)


def modes_kernel(sizes, split, scale, back_scale, sources, place, col_table, back_table, ids, bands, *refs):
    slots, reals, groups, width, fold, virtual, per = sizes
    parts, (low_out, *outs) = refs[:sources], refs[sources:]
    ch = low_out.shape[1]
    share = low_out.shape[0] // 4
    here = parts[0].shape[0] // (2 * virtual)
    cols_dev = outs[0].shape[0] // (2 * here)
    first = place[0] * slots + (place[1] * here if split else 0)

    def bands_of(row, rows, begin):
        line = jnp.broadcast_to(ids[pl.ds(row, 1), :], (rows, KW))
        wanted = lax.broadcasted_iota(jnp.int32, (rows, KW), 0) % KW + begin
        at = lax.broadcasted_iota(jnp.int32, (rows, KW), 1)
        return jnp.sum(jnp.where(wanted == at, line, 0).astype(F32), axis=1, keepdims=True)

    low_line = bands_of(0, share, place[0] * share)
    for s in range(here):
        blocks = [part[2 * s * virtual : 2 * (s + 1) * virtual].astype(F32) for part in parts]
        cosine = jnp.concatenate([block[:virtual] for block in blocks], axis=0)
        sine = jnp.concatenate([block[virtual:] for block in blocks], axis=0)
        cells = jnp.concatenate([cosine, sine], axis=1).astype(BF16)
        freqs = jnp.dot(col_table[...], cells, preferred_element_type=F32)
        over_cos, over_sin = freqs[:KW], freqs[KW:]
        slot = first + s
        plus = jnp.where(slot == 0, 0.0, scale)
        low = sum(blocks)
        coefs = jnp.concatenate(
            [
                (over_cos[:, :ch] - over_sin[:, ch:]) * plus,
                (over_cos[:, :ch] + over_sin[:, ch:]) * scale,
                (over_cos[:, ch:] + over_sin[:, :ch]) * plus,
                (over_sin[:, :ch] - over_cos[:, ch:]) * scale,
                low[width : width + share] * scale,
                low[virtual + width : virtual + width + share] * scale,
                jnp.zeros((2 * share, ch), F32),
            ],
            axis=0,
        ).astype(BF16)
        wide = coefs.astype(F32)
        plus_line = bands_of(slot, KW, 0)
        minus_line = bands_of(jnp.where(slot == 0, KH // 2, KH - slot), KW, 0)
        band = jnp.concatenate([plus_line, minus_line, plus_line, minus_line] + [low_line] * 4, axis=0)
        mixed = None
        for b in range(bands.shape[0]):
            chosen = jnp.where(band == float(b), wide, 0.0).astype(BF16)
            part = lax.dot_general(chosen, bands[b], NT, preferred_element_type=F32)
            mixed = part if mixed is None else mixed + part
        mixed = (mixed * back_scale).astype(BF16)
        if s == 0:
            low_out[...] = mixed[4 * KW :]
        plus_cos, minus_cos = mixed[:KW], mixed[KW : 2 * KW]
        plus_sin, minus_sin = mixed[2 * KW : 3 * KW], mixed[3 * KW : 4 * KW]
        sides = jnp.concatenate(
            [
                jnp.concatenate([plus_cos, plus_sin, minus_cos, minus_sin], axis=0),
                jnp.concatenate([plus_sin, -plus_cos, -minus_sin, minus_cos], axis=0),
            ],
            axis=1,
        )
        field = jnp.dot(back_table[...], sides, preferred_element_type=F32).astype(BF16)
        for z, out in enumerate(outs):
            span = slice(z * cols_dev, (z + 1) * cols_dev)
            begin = 2 * s * cols_dev
            out[begin : begin + cols_dev] = field[span, :ch]
            out[begin + cols_dev : begin + 2 * cols_dev] = field[span, ch:]


def final_kernel(count, main, edges, spans, place, tables, grad_far, left, right, above, below, *refs):
    blocks, (out_far, out, grad, rows, cells, lcol, rcol, sem, out_sems) = refs[:count], refs[count:]
    rows_dev, cols_dev, ch = out.shape
    apart = pitch(cols_dev)
    table, low_table = tables[spans[0]], tables[spans[1]]
    depth = table.shape[1]
    valid = neighbours(place, edges)
    grad_copy = pltpu.make_async_copy(grad_far, grad, sem)
    grad_copy.start()
    for place, block in enumerate(blocks):
        for i in range(main // cols_dev):
            line = block[i * cols_dev : (i + 1) * cols_dev].astype(F32)
            set_rows(rows, (place * (main // cols_dev) + i) * apart, line)
    used = count * (main // cols_dev)
    low = jnp.concatenate([block[main:] for block in blocks], axis=0)
    set_rows(rows, used * apart, jnp.dot(low_table, low, preferred_element_type=F32))
    set_rows(rows, (used + 1) * apart, jnp.zeros((rows.shape[1] - (used + 1) * apart, ch), F32))
    lcol[...] = left[left.shape[0] - rows_dev :].astype(F32) * valid[0]
    rcol[...] = right[right.shape[0] - rows_dev :].astype(F32) * valid[1]
    for w in range(0, cols_dev, 2):
        modes = jnp.concatenate(
            [get_rows(rows, w + i, depth, apart).astype(BF16) for i in range(2)], axis=1
        )
        lines = jnp.dot(table, modes, preferred_element_type=F32)
        for i in range(2):
            set_rows(cells, w + i, lines[:, i * ch : (i + 1) * ch], apart)
    column = lax.broadcasted_iota(jnp.int32, (cols_dev, ch), 0)

    def total(at):
        line = get_rows(cells, pl.multiple_of(at * apart, 8), cols_dev) + grad[at]
        line = line + jnp.where(column == 0, lcol[pl.ds(at, 1), :], 0.0)
        return line + jnp.where(column == cols_dev - 1, rcol[pl.ds(at, 1), :], 0.0)

    grad_copy.wait()

    def store(step, carry):
        for sub in range(4):
            at = step * 4 + sub
            out[at] = total(at).astype(BF16)
        return carry

    last = rows_dev - 1
    copies = []
    for i in range(rows_dev // TILE):
        lax.fori_loop(i * TILE // 4, (i + 1) * TILE // 4, store, 0)
        if i == 0:
            out[0] = (total(0) + above[...].astype(F32)).astype(BF16)
        if (i + 1) * TILE == rows_dev:
            out[last] = (total(last) + below[...].astype(F32)).astype(BF16)
        span = pl.ds(i * TILE, TILE)
        copies.append(pltpu.make_async_copy(out.at[span], out_far.at[span], out_sems.at[i]))
        copies[-1].start()
    for copy in copies:
        copy.wait()


def in_vmem():
    return pl.BlockSpec(memory_space=pltpu.VMEM)


def in_hbm():
    return pl.BlockSpec(memory_space=pltpu.HBM)


def in_smem():
    return pl.BlockSpec(memory_space=pltpu.SMEM)


def call(kernel, out_shapes, in_specs, scratch, name, limit, out_specs=None):
    many = isinstance(out_shapes, (list, tuple))
    return pl.pallas_call(
        kernel,
        out_shape=out_shapes,
        in_specs=in_specs,
        out_specs=out_specs or ([in_vmem() for _ in out_shapes] if many else in_vmem()),
        scratch_shapes=scratch,
        compiler_params=pltpu.CompilerParams(vmem_limit_bytes=limit << 20),
        name=name,
    )


def cos_sin(product, period):
    theta = (product % period) * (2.0 * math.pi / period)
    return np.cos(theta), np.sin(theta)


def padded(table, rows, cols):
    return np.pad(table, ((0, rows - table.shape[0]), (0, cols - table.shape[1])))


def angle_tables(n_gx, n_gy, rows_dev, cols_dev):
    sizes = layout(n_gx, cols_dev)
    slots, reals, groups, width, fold, virtual, per = sizes
    chips, share = n_gx // 2, KW // n_gx
    split = slots % n_gy == 0
    here = slots // n_gy if split else slots
    full_rows, full_cols = rows_dev * n_gx, cols_dev * n_gy
    used = 2 * chips * reals
    depth_in, depth_out = round_up(rows_dev + 2, 16), round_up(used + 1, 16)
    modes = np.arange(KW)
    chip_ids = np.arange(chips)

    def row_angles(rows, freqs):
        cosine, sine = cos_sin(rows[:, None] * freqs[None, :], full_rows)
        table = np.stack([cosine, sine], axis=2).reshape(len(rows), used)
        ones = np.ones((len(rows), 1))
        return np.concatenate([table, ones, np.zeros((len(rows), depth_out - used - 1))], axis=1)

    def low_angles(cols, owners):
        product = (owners[:, None] * share + np.arange(share)[None, :])[None] * cols[:, None, None]
        cosine, sine = cos_sin(product, full_cols)
        spare = np.zeros_like(cosine)
        return np.concatenate([cosine, sine, spare, spare], axis=2)

    def owners_of(order, core):
        return np.concatenate([2 * order + core, 2 * order + 1 - core])

    both, forth, back = [], [], []
    wide = np.arange(virtual)
    for gy in range(n_gy):
        sources = (gy - np.arange(n_gy)) % n_gy if split else np.arange(n_gy)
        ext_cols = sources[:, None] * cols_dev - 1 + wide[None, :]
        inside = (ext_cols >= 0) & (ext_cols < full_cols) & (wide < width)[None, :]
        cosine, sine = cos_sin(modes[:, None] * ext_cols.reshape(1, -1), full_cols)
        forth.append(np.concatenate([cosine, sine]) * inside.reshape(1, -1))
        all_cols = (sources[:, None] * cols_dev + np.arange(cols_dev)[None, :]).reshape(-1, 1)
        back.append(np.concatenate(cos_sin(all_cols * modes[None, :], full_cols) * 2, axis=1))
    for gx in range(n_gx):
        chip, core = gx // 2, gx % 2
        for gy in range(n_gy):
            places = np.arange(slots)
            if split:
                places = (places + gy * here) % slots

            def frequencies(owners):
                ids = (owners[:, None] * slots + places[None, :]).reshape(-1)
                return np.where(ids == 0, KH // 2, ids)

            order = (chip_ids + chip) % chips
            ext_rows = gx * rows_dev - 1 + np.arange(depth_in)
            inside = (ext_rows >= 0) & (ext_rows < full_rows) & (np.arange(depth_in) < rows_dev + 2)
            row_table = (row_angles(ext_rows, frequencies(owners_of(order, core))) * inside[:, None]).T
            owners = owners_of((chip - chip_ids) % chips, core)
            back_rows = row_angles(gx * rows_dev + np.arange(rows_dev), frequencies(owners))
            cols = gy * cols_dev - 1 + wide
            inside = (cols >= 0) & (cols < full_cols) & (wide < width)
            low_table = (low_angles(cols, np.array([gx]))[:, 0] * inside[:, None]).T
            back_low = low_angles(gy * cols_dev + np.arange(cols_dev), owners).reshape(cols_dev, -1)
            tables = [row_table, back_rows, low_table, back_low]
            lanes = round_up(max(table.shape[1] for table in tables), LANES)
            both.append(np.concatenate([padded(t, round_up(len(t), 16), lanes) for t in tables]))
    both = np.stack(both).reshape(n_gx, n_gy, *both[0].shape)
    return [np.asarray(table, np.float32).astype(BF16) for table in (both, np.stack(forth), np.stack(back))]


def table_spans(sizes, rows_dev, cols_dev, n_gx):
    slots, reals, groups, width, fold, virtual, per = sizes
    used, share = n_gx * reals, KW // n_gx
    shapes = [
        (round_up(used + 1, 16), round_up(rows_dev + 2, 16)),
        (rows_dev, round_up(used + 1, 16)),
        (4 * share, virtual),
        (cols_dev, n_gx * 4 * share),
    ]
    spans, begin = [], 0
    for rows, cols in shapes:
        spans.append((slice(begin, begin + rows), slice(0, cols)))
        begin += round_up(rows, 16)
    return spans


def body(saved_mid, out_grad, expert_weight, routes, gates, band_matrix, band_ids):
    rows_dev, cols_dev, ch = saved_mid.shape
    n_gx, n_gy = lax.axis_size("gx"), lax.axis_size("gy")
    gx, gy = lax.axis_index("gx"), lax.axis_index("gy")
    full_rows, full_cols = rows_dev * n_gx, cols_dev * n_gy
    sizes = layout(n_gx, cols_dev)
    slots, reals, groups, width, fold, virtual, per = sizes
    chips = n_gx // 2
    swap = [(i, i ^ 1) for i in range(n_gx)]
    experts = expert_weight.shape[0]

    def ring(array, axis, step):
        count = lax.axis_size(axis)
        return lax.ppermute(array, axis, [(i, (i + step) % count) for i in range(count)])

    def shape(*dims, dtype=BF16):
        return jax.ShapeDtypeStruct(dims, dtype)

    split = slots % n_gy == 0
    here = slots // n_gy if split else slots
    depth_in, depth_out = round_up(rows_dev + 2, 16), round_up(n_gx * reals + 1, 16)
    spans = table_spans(sizes, rows_dev, cols_dev, n_gx)
    tables, col_tables, back_tables = angle_tables(n_gx, n_gy, rows_dev, cols_dev)
    tables = jnp.asarray(tables)[gx, gy]
    col_table, back_table = jnp.asarray(col_tables)[gy], jnp.asarray(back_tables)[gy]
    share = KW // n_gx
    place = jnp.stack([gx, gy]).astype(jnp.int32)
    edges = (n_gx, n_gy)

    left = ring(saved_mid[:, cols_dev - 1, :], "gy", 1)
    right = ring(saved_mid[:, 0, :], "gy", -1)

    def edge_row(at):
        return jnp.concatenate([saved_mid[at], left[at : at + 1], right[at : at + 1]], axis=0)

    bottom = ring(edge_row(0), "gx", -1)
    top = ring(edge_row(rows_dev - 1), "gx", 1)

    picked = routes.shape[2]
    packed = per * ch
    lines = edge_blocks(cols_dev)
    extra = -(-2 * lines // chips) * ch
    keep, give, grad, e_left, e_right = call(
        functools.partial(conv_kernel, sizes, picked, edges, spans[0]),
        [
            shape(chips, groups * reals, packed),
            shape(chips, groups * reals, packed + extra),
            pltpu.HBM((rows_dev, cols_dev, ch), F32),
            shape(rows_dev, ch),
            shape(rows_dev, ch),
        ],
        [in_smem()] * 3 + [in_hbm()] + [in_vmem()] * 4 + [in_hbm()] * 2 + [in_vmem()],
        [
            pltpu.VMEM((rows_dev, cols_dev, ch), BF16),
            pltpu.VMEM((rows_dev, cols_dev, ch), BF16),
            pltpu.VMEM((experts, 9 * ch, ch), BF16),
            pltpu.VMEM((rows_dev, cols_dev, ch), F32),
            pltpu.VMEM((3, rows_dev + 2, cols_dev, ch), BF16),
            pltpu.VMEM((TILE * TILE, 9 * ch), BF16),
            pltpu.VMEM((TILE * TILE, (SHARED + picked) * ch), BF16),
            pltpu.VMEM((TILE * TILE, (SHARED + picked) * ch), BF16),
            pltpu.VMEM((3, rows_dev + 2, cols_dev, ch), F32),
            planes(depth_in * virtual, ch),
            planes(round_up(max(width, reals * fold), 8), ch),
            pltpu.VMEM((rows_dev, ch), F32),
            pltpu.VMEM((rows_dev, ch), F32),
            pltpu.SemaphoreType.DMA((experts,)),
            pltpu.SemaphoreType.DMA((2 + rows_dev // TILE,)),
        ],
        "conv",
        40,
        [in_vmem()] * 2 + [in_hbm()] + [in_vmem()] * 2,
    )(
        routes.reshape(-1),
        gates.reshape(-1),
        place,
        pltpu.with_memory_space_constraint(saved_mid, pltpu.HBM),
        left,
        right,
        top,
        bottom,
        pltpu.with_memory_space_constraint(out_grad, pltpu.HBM),
        pltpu.with_memory_space_constraint(expert_weight.reshape(experts, 9 * ch, ch), pltpu.HBM),
        tables,
    )

    gift = lax.ppermute(give, "gx", swap)
    messages = [(keep[d].astype(F32) + gift[d, :, :packed].astype(F32)).astype(BF16) for d in range(chips)]
    for d, which in ((1, 1), (chips - 1, 0)):
        edge = find_edge(gift, chips, per, ch, lines, which)
        messages[d] = jnp.concatenate([messages[d], edge], axis=1)
    parts = [messages[0]] + [ring(messages[d], "gx", 2 * d) for d in range(1, chips)]
    block_rows = here * 2 * virtual
    if split:
        ends = [rows_dev if d in (1, n_gy - 1) else 0 for d in range(n_gy)]
        regrouped = [shape(block_rows + end, ch) for end in ends]
    else:
        regrouped = [shape(block_rows, ch), shape(rows_dev, ch), shape(rows_dev, ch)]
    from_above, from_below, *regrouped = call(
        functools.partial(regroup_kernel, sizes, chips, here, edges, spans[2]),
        [shape(cols_dev, ch), shape(cols_dev, ch), *regrouped],
        [in_smem()] + [in_vmem()] * (4 + chips),
        [planes((reals + 1) * virtual, ch)],
        "regroup",
        8,
    )(place, gift, e_left, e_right, tables, *parts)

    if split:
        cells = [regrouped[0]] + [ring(regrouped[d], "gy", d) for d in range(1, n_gy)]
        from_left, from_right = cells[1], cells[n_gy - 1]
    else:
        gathered = lax.all_gather(regrouped[0], "gy", axis=0)
        cells = [gathered[z] for z in range(n_gy)]
        from_left, from_right = ring(regrouped[1], "gy", 1), ring(regrouped[2], "gy", -1)
    low_modes, *mixed = call(
        functools.partial(
            modes_kernel,
            sizes,
            split,
            1.0 / math.sqrt(full_rows * full_cols),
            1.0 / math.sqrt(2 * KH * KW),
            n_gy,
        ),
        [shape(4 * share, ch)] + [shape(here * 2 * cols_dev, ch) for _ in range(n_gy)],
        [in_smem()] + [in_vmem()] * (4 + n_gy),
        [],
        "modes",
        12,
    )(place, col_table, back_table, band_ids, band_matrix, *cells)
    if split:
        mixed = [mixed[0]] + [ring(mixed[d], "gy", -d) for d in range(1, n_gy)]
    else:
        mixed = [lax.dynamic_index_in_dim(jnp.stack(mixed), gy, 0, keepdims=False)]
    block = jnp.concatenate([*mixed, low_modes], axis=0)

    blocks = [block] + [ring(block, "gx", 2 * d) for d in range(1, chips)]
    blocks = blocks + [lax.ppermute(array, "gx", swap) for array in blocks]
    return call(
        functools.partial(final_kernel, n_gx, slots * 2 * cols_dev, edges, (spans[1], spans[3])),
        shape(rows_dev, cols_dev, ch),
        [in_smem(), in_vmem(), in_hbm()] + [in_vmem()] * (4 + n_gx),
        [
            pltpu.VMEM((rows_dev, cols_dev, ch), BF16),
            pltpu.VMEM((rows_dev, cols_dev, ch), F32),
            planes(depth_out * pitch(cols_dev), ch),
            planes(rows_dev * pitch(cols_dev), ch),
            pltpu.VMEM((rows_dev, ch), F32),
            pltpu.VMEM((rows_dev, ch), F32),
            pltpu.SemaphoreType.DMA,
            pltpu.SemaphoreType.DMA((rows_dev // TILE,)),
        ],
        "final",
        16,
        in_hbm(),
    )(place, tables, grad, from_left, from_right, from_above, from_below, *blocks)


def solution(mesh):
    placed = (
        P("gx", "gy", None),
        P("gx", "gy", None),
        P(),
        P("gx", "gy", None),
        P("gx", "gy", None),
        P(),
        P(),
    )
    return jax.shard_map(
        body, mesh=mesh, in_specs=placed, out_specs=P("gx", "gy", None), check_vma=False
    )
```
